512 devices in a mesh: rows: 64 (over z, y), rep: 8 (over x, core).
Axes of the slice: x: 4, y: 8, z: 8, core: 2. Of those that a mesh axis runs over, the one named last changes fastest.
Arguments:
- nodes: bfloat16 [8192, 512], P('rows'), may hold values from -6 to 6
- adjacency: bfloat16 [8192, 8192], P('rows', 'rep'), may hold values from 0 to 2, as said below
- gain: float32 [512], replicated, may hold values from 0.1 to 1.9
- w_in: bfloat16 [512, 512], replicated, may hold values from -0.25 to 0.25
- w_out: bfloat16 [512, 512], replicated, may hold values from -0.25 to 0.25
- cotangent: bfloat16 [8192, 512], P('rows'), may hold values from -2 to 2
Outputs:
- node_out: bfloat16 [8192, 512], P('rows')
- node_grad: bfloat16 [8192, 512], P('rows')
- grad_w_in: float32 [512, 512], replicated
- grad_w_out: float32 [512, 512], replicated
- grad_gain: float32 [512], replicated
The draws below stay inside these ranges and needn't reach their ends.
Inputs may be any that keep to these rules, and one draw needn't show every extreme that they name: adjacency holds whole numbers, is symmetric, every diagonal entry is 1, and off the diagonal it is zero outside a set of live 128 x 128 blocks.
All inputs are finite; a program needn't handle non-finite values.
Results may differ from the reference program's by a relative error of at most 0.0054.
Values may be sent and summed in bfloat16 or wider, within the bound.
No kernel may reach another device: no remote copies, remote signals or barrier semaphores. Data moves between devices by JAX's collectives and lax.ppermute only.
A program may use at most 64 MiB of HBM per device.

```python
import jax
import jax.numpy as jnp
from jax import lax

D = 512
BLOCK = 128
GROUP_ROWS = 128
NODES = 8192
N_ROWS = 64


def draw_adjacency(key, part):
    key = jax.random.fold_in(key, 11)
    key_hot, key_live, key_seed = jax.random.split(key, 3)
    blocks = NODES // BLOCK
    hotness = jax.random.randint(key_hot, (blocks,), 1, 6)
    chance = jax.random.randint(key_live, (blocks, blocks), 0, 160)
    chance = jnp.minimum(chance, chance.T)
    block_ids = jnp.arange(blocks, dtype=jnp.int32)
    live = (chance < hotness[:, None] * hotness[None, :]) | (jnp.abs(block_ids[:, None] - block_ids[None, :]) <= 1)
    live_full = jnp.repeat(jnp.repeat(live, BLOCK, axis=0), BLOCK, axis=1)
    seed_value = jax.random.randint(key_seed, (), 0, 1048576)
    index = jnp.arange(NODES, dtype=jnp.int32)
    product = index[:, None] * index[None, :]
    total = index[:, None] + index[None, :]
    mixed = product * 40503 + total * 9973 + seed_value
    mixed = jnp.bitwise_xor(mixed, jnp.right_shift(mixed, 15))
    mixed = mixed * 2246822
    mixed = jnp.bitwise_xor(mixed, jnp.right_shift(mixed, 13))
    pattern = jnp.bitwise_and(jnp.right_shift(mixed, 4), 15)
    multiple = jnp.where(pattern == 0, 2.0, jnp.where(pattern < 3, 1.0, 0.0))
    multiple = jnp.where(live_full, multiple, 0.0)
    diagonal = index[:, None] == index[None, :]
    return jnp.where(diagonal, 1.0, multiple).astype(jnp.float32).astype(jnp.bfloat16)


def level_of(own_key, dims, cuts, least, largest):
    def one(dim, blocks):
        steps = jax.random.uniform(jax.random.fold_in(jax.random.fold_in(own_key, 6), dim), (blocks,), jnp.float32, least / len(cuts), largest / len(cuts))
        return jnp.repeat(jnp.exp(steps), dims[dim] // blocks).reshape((-1,) + (1,) * (len(dims) - dim - 1))

    level = one(*cuts[0])
    for cut in cuts[1:]:
        level = level * one(*cut)
    return level


def noise(stream_key, dims, deviation, limit, shards=(), held_as=jnp.bfloat16):
    loudness = level_of(stream_key, dims, shards, -0.22, 0.18) if shards else 1.0
    result = jax.random.normal(stream_key, dims, jnp.float32) * deviation * loudness
    return jnp.minimum(jnp.maximum(result, -limit), limit).astype(held_as)


def setup_inputs(seed: int = 0) -> dict:
    arg_keys = jax.random.split(jax.random.key(seed), 7)
    return {
        "nodes": noise(arg_keys[0], (NODES, D), 1.0, 6.0, ((0, 64),)),
        "adjacency": draw_adjacency(jax.random.fold_in(arg_keys[6], 71), 0),
        "gain": jnp.clip(1.0 + 0.18 * jax.random.normal(arg_keys[2], (D,), jnp.float32), 0.1, 1.9),
        "w_in": noise(arg_keys[3], (D, D), D ** -0.5, 0.25),
        "w_out": noise(arg_keys[4], (D, D), D ** -0.5, 0.25),
        "cotangent": noise(arg_keys[5], (NODES, D), 0.125, 2.0, ((0, 64),)),
    }


def aggregate(adjacency, field):
    field_wide = field.astype(jnp.float32)
    slabs = adjacency.reshape(N_ROWS, GROUP_ROWS, NODES)

    def one_slab(slab):
        return jnp.dot(slab.astype(jnp.float32), field_wide, precision=lax.Precision.HIGHEST)
    return lax.map(one_slab, slabs).reshape(NODES, field.shape[1])

def reference(nodes, adjacency, gain, w_in, w_out, cotangent):
    summed = aggregate(adjacency, nodes)
    scale = lax.rsqrt(lax.optimization_barrier(jnp.mean(summed * summed, axis=-1, keepdims=True)) + 1e-05)
    normed = summed * scale
    lifted = (normed * gain).astype(jnp.bfloat16)
    pre = jnp.dot(lifted, w_in, preferred_element_type=jnp.float32)
    sigma = jax.nn.sigmoid(pre)
    hidden = (pre * sigma).astype(jnp.bfloat16)
    node_out = (nodes.astype(jnp.float32) + jnp.dot(hidden, w_out, preferred_element_type=jnp.float32)).astype(jnp.bfloat16)
    grad_hidden = jnp.dot(cotangent, w_out.T, preferred_element_type=jnp.float32)
    grad_pre = (grad_hidden * sigma * (1.0 + pre * (1.0 - sigma))).astype(jnp.bfloat16)
    grad_w_out = jnp.dot(hidden.T, cotangent, preferred_element_type=jnp.float32)
    grad_w_in = jnp.dot(lifted.T, grad_pre, preferred_element_type=jnp.float32)
    grad_lifted = jnp.dot(grad_pre, w_in.T, preferred_element_type=jnp.float32)
    grad_gain = lax.optimization_barrier(jnp.sum(grad_lifted * normed, axis=0))
    grad_normed = grad_lifted * gain
    grad_summed = (scale * (grad_normed - normed * lax.optimization_barrier(jnp.mean(grad_normed * normed, axis=-1, keepdims=True)))).astype(jnp.bfloat16)
    node_grad = (cotangent.astype(jnp.float32) + aggregate(adjacency, grad_summed)).astype(jnp.bfloat16)
    return (node_out, node_grad, grad_w_in, grad_w_out, grad_gain)
```

```python
import jax
import jax.numpy as jnp
from jax import lax
from jax.sharding import PartitionSpec as P

BF = jnp.bfloat16
F32 = jnp.float32
NR = 64
NP = 8
S = 16


def index(z, y, p):
    return (z * 8 + y) * NP + p


TRIPLES = [(z, y, p) for z in range(8) for y in range(8) for p in range(8)]
OUT = [(index(z, y, p), index(y, p, z)) for z, y, p in TRIPLES]
BACK = [(b, a) for a, b in OUT]


def dot(a, b, ca, cb):
    return lax.dot_general(a, b, (((ca,), (cb,)), ((), ())), preferred_element_type=F32)


def spread(x, axis, n):
    return lax.all_to_all(jnp.broadcast_to(x, (n,) + x.shape), axis, 0, 0)


def shards(nodes, adjacency, gain, w_in, w_out, cotangent):
    p = lax.axis_index("rep")
    own = lambda a: lax.dynamic_slice_in_dim(a, p * S, S, 0)
    cot_piece = own(cotangent)
    moved = lax.ppermute(jnp.stack([own(nodes), cot_piece]), ("rows", "rep"), OUT)
    x, cot = moved[0], moved[1]

    part = dot(adjacency, nodes, 0, 0).astype(BF).reshape(NR, S, 512)
    got = lax.all_to_all(part, "rows", 0, 0)
    summed = jnp.sum(got.astype(F32), axis=0)

    scale = lax.rsqrt(jnp.mean(summed * summed, axis=-1, keepdims=True) + 1e-05)
    normed = summed * scale
    lifted = (normed * gain).astype(BF)
    pre = dot(lifted, w_in, 1, 0)
    sigma = jax.nn.sigmoid(pre)
    hidden = (pre * sigma).astype(BF)
    node_out = (x.astype(F32) + dot(hidden, w_out, 1, 0)).astype(BF)
    grad_hidden = dot(cot, w_out, 1, 1)
    grad_pre = (grad_hidden * sigma * (1.0 + pre * (1.0 - sigma))).astype(BF)
    grad_lifted = dot(grad_pre, w_in, 1, 1)
    gain_part = jnp.sum(grad_lifted * normed, axis=0)
    grad_normed = grad_lifted * gain
    grad_summed = (
        scale * (grad_normed - normed * jnp.mean(grad_normed * normed, axis=-1, keepdims=True))
    ).astype(BF)

    field = spread(grad_summed, "rows", NR).reshape(NR * S, 512)
    back = dot(adjacency, field, 1, 0).reshape(NP, S, 512)

    acts = jnp.stack(
        [
            jnp.concatenate(
                [lifted[:, 128 * i : 128 * i + 128], hidden[:, 128 * i : 128 * i + 128],
                 grad_pre[:, 256 * c : 256 * c + 256], cot[:, 256 * c : 256 * c + 256]], axis=1)
            for i in range(4) for c in range(2)
        ]
    )
    acts = lax.all_to_all(acts, "rep", 0, 0).reshape(NP * S, 768)
    w2 = jnp.concatenate(
        [dot(acts[:, 0:128], acts[:, 256:512], 0, 0), dot(acts[:, 128:256], acts[:, 512:768], 0, 0)], axis=0
    )
    blocks = w2.reshape(32, 8, 2, 128).transpose(0, 2, 1, 3).reshape(NR, 8, 128)
    gain_rows = jnp.broadcast_to(jnp.pad(gain_part.reshape(4, 128), ((0, 4), (0, 0))), (NR, 8, 128))
    terms = jnp.concatenate([blocks, gain_rows], axis=1).astype(BF)
    terms = jnp.sum(lax.all_to_all(terms, "rows", 0, 0).astype(F32), axis=0)
    mine = spread(terms[:8].astype(BF), "rows", NR)

    back = lax.all_to_all(back, "rep", 0, 0)
    node_grad = (cot_piece.astype(F32) + jnp.sum(back, axis=0)).astype(BF)

    node_out = lax.ppermute(node_out, ("rows", "rep"), BACK)
    gain_row = jnp.pad(terms[8:12].reshape(1, 512), ((0, 15), (0, 0))).astype(BF)
    table = mine.reshape(16, 4, 8, 128).transpose(0, 2, 1, 3).reshape(128, 512)
    last = spread(jnp.concatenate([table, node_grad, node_out, gain_row], axis=0), "rep", NP)
    node_grad = last[:, 128:144].reshape(128, 512)
    node_out = last[:, 144:160].reshape(128, 512)
    grad_gain = jnp.sum(last[:, 160].astype(F32), axis=0)
    w2 = last[:, :128].reshape(4, 2, 16, 8, 4, 128).transpose(0, 1, 2, 4, 3, 5).reshape(4, 2, 2, 16, 2, 8, 128)
    w2 = w2.transpose(2, 0, 3, 5, 1, 4, 6).reshape(2, 512, 512).astype(F32)
    return (node_out, node_grad, w2[0], w2[1], grad_gain)


def solution(mesh):
    return jax.shard_map(
        shards,
        mesh=mesh,
        in_specs=(P("rows", None), P("rows", "rep"), P(), P(), P(), P("rows", None)),
        out_specs=(P("rows", None), P("rows", None), P(), P(), P()),
        check_vma=False,
    )
```

```python
import jax
import jax.numpy as jnp
from jax import lax
from jax.experimental import pallas as pl
from jax.experimental.pallas import tpu as pltpu
from jax.sharding import PartitionSpec as P


BF = jnp.bfloat16
F32 = jnp.float32
ALL = ("rows", "rep")


def place(u, v, p):
    z, y = (v, u) if p % 2 == 0 else (u, v)
    return (8 * z + y) * 8 + p


E8 = range(8)
ALONG_U = [[place(u, v, p) for u in E8] for v in E8 for p in E8]
ALONG_V = [[place(u, v, p) for v in E8] for u in E8 for p in E8]
ALONG_X = [[r * 8 + 2 * x + c for x in range(4)] for r in range(64) for c in range(2)]
OUT = [((8 * z + y) * 8 + t, place(t, y, z)) for z in E8 for y in E8 for t in E8]
BACK = [(b, a) for a, b in OUT]
CORE = [(i, i ^ 1) for i in range(512)]


def dot(a, b, ca, cb):
    return lax.dot_general(a, b, (((ca,), (cb,)), ((), ())), preferred_element_type=F32)


def trade(x, groups):
    return lax.all_to_all(x, ALL, 0, 0, axis_index_groups=groups)


def call(body, outs, *args, scalar=None):
    specs = [pl.BlockSpec(memory_space=pltpu.VMEM)] * len(args)
    if scalar is not None:
        args = (scalar,) + args
        specs = [pl.BlockSpec(memory_space=pltpu.SMEM)] + specs
    return pl.pallas_call(
        body,
        out_shape=[jax.ShapeDtypeStruct(s, d) for s, d in outs],
        in_specs=specs,
        out_specs=[pl.BlockSpec(memory_space=pltpu.VMEM)] * len(outs),
        compiler_params=pltpu.CompilerParams(vmem_limit_bytes=40 * 1024 * 1024),
    )(*args)


def left_half():
    return lax.broadcasted_iota(jnp.int32, (1, 128), 1) < 64


def update(c_ref, got, gain_ref, w_in_ref, w_out_ref, moved, out_ref, send, gain_part):
    summed = got[0]
    for i in range(1, 8):
        summed = summed + got[i]
    gain = gain_ref[...]
    w_in, w_out = w_in_ref[...], w_out_ref[...]
    cot = moved[1]
    scale = lax.rsqrt(jnp.mean(summed * summed, axis=-1, keepdims=True) + 1e-05)
    normed = summed * scale
    lifted = (normed * gain).astype(BF)
    pre = dot(lifted, w_in, 1, 0)
    grad_hidden = dot(cot, w_out, 1, 1)
    sigma = jax.nn.sigmoid(pre)
    hidden = (pre * sigma).astype(BF)
    grad_pre = (grad_hidden * sigma * (1.0 + pre * (1.0 - sigma))).astype(BF)
    grad_lifted = dot(grad_pre, w_in, 1, 1)
    out_ref[...] = (moved[0].astype(F32) + dot(hidden, w_out, 1, 0)).astype(BF)
    gain_row = jnp.sum(grad_lifted * normed, axis=0, keepdims=True)
    gain_part[...] = jnp.zeros_like(gain_part)
    for j in range(4):
        gain_part[j : j + 1, :] = gain_row[:, 128 * j : 128 * j + 128]
    grad_normed = grad_lifted * gain
    grad_summed = (
        scale * (grad_normed - normed * jnp.mean(grad_normed * normed, axis=-1, keepdims=True))
    ).astype(BF)
    for u in E8:
        send[u, :, 0:512] = grad_summed
    left = left_half()
    first = c_ref[0] == 0

    def pairs(a, b):
        a, b = a.astype(F32), b.astype(F32)
        blocks = []
        for m in range(4):
            one, two = a[:, 128 * m : 128 * m + 128], b[:, 128 * m : 128 * m + 128]
            blocks.append(jnp.where(left, one, pltpu.roll(two, 64, 1)))
            blocks.append(jnp.where(left, pltpu.roll(one, 64, 1), two))
        return blocks

    rows, columns = pairs(lifted, hidden), pairs(grad_pre, cot)
    for k in E8:
        by_v = jnp.where(first, rows[k], columns[k]).astype(BF)
        by_u = jnp.where(first, columns[k], rows[k]).astype(BF)
        for u in E8:
            send[u, :, 512 + 128 * k : 640 + 128 * k] = by_v
        send[k, :, 1536:1664] = by_u


def forward_on(got, send):
    for u in E8:
        field, by_u = got[u, :, 0:512], got[u, :, 1536:1664]
        for v in E8:
            send[v, 16 * u : 16 * u + 16, 0:512] = field
            send[v, 16 * u : 16 * u + 16, 512:640] = got[u, :, 512 + 128 * v : 640 + 128 * v]
            send[v, 16 * u : 16 * u + 16, 640:768] = by_u


def back_and_tile(c_ref, adjacency, got, gain_part, send):
    table = got[...].reshape(1024, 768)
    back = dot(adjacency[...], table[:, 0:512], 1, 0)
    for q in E8:
        for j in range(4):
            send[q, 16 * j : 16 * j + 16, :] = back[16 * q : 16 * q + 16, 128 * j : 128 * j + 128]
    by_v, by_u = table[:, 512:640], table[:, 640:768]
    first = c_ref[0] == 0
    rows = jnp.where(first, by_v, by_u)
    columns = jnp.where(first, by_u, by_v)
    tile = dot(rows, columns, 0, 0)
    tile = jnp.where(left_half(), tile[0:64], tile[64:128])
    part = gain_part[...]
    for q in E8:
        send[q, 64:72, :] = tile[8 * q : 8 * q + 8]
        send[q, 72:80, :] = part


def add_up(p_ref, got, cotangent, grad, send):
    total = got[0]
    for i in range(1, 8):
        total = total + got[i]
    own = cotangent[pl.ds(pl.multiple_of(p_ref[0] * 16, 16), 16), :].astype(F32)
    for j in range(4):
        grad[16 * j : 16 * j + 16, :] = (
            own[:, 128 * j : 128 * j + 128] + total[16 * j : 16 * j + 16]
        ).astype(BF)
    block = total[64:80].astype(BF)
    for u in E8:
        send[u] = block


def pack(got, grad, out, send, gain):
    total = jnp.zeros((8, 128), F32)
    for i in range(32):
        one, two = got[2 * i].astype(F32), got[2 * i + 1].astype(F32)
        total = total + one[8:16] + two[8:16]
        both = jnp.concatenate([one[0:8], two[0:8]], axis=0).astype(BF)
        for x in range(4):
            send[x, 16 * i : 16 * i + 16, :] = both
    gain[...] = total
    grad = grad[...]
    for x in range(4):
        send[x, 512:576, :] = grad
        for j in range(4):
            send[x, 576 + 16 * j : 592 + 16 * j, :] = out[:, 128 * j : 128 * j + 128]


def unpack(c_ref, mine, other, grad_in, grad_out, node_grad, node_out):
    left = left_half()

    def lay(src, c):
        for x in range(4):
            q = 2 * x + c
            for z in E8:
                at = slice(64 * z + 8 * q, 64 * z + 8 * q + 8)
                for m in range(4):
                    if c == 0:
                        both = src[x, 64 * z + 16 * m : 64 * z + 16 * m + 16, :].astype(F32)
                        even, odd = both[0:8], both[8:16]
                    else:
                        k, half = 8 * (z // 2) * 2, 8 * (z % 2)
                        even = src[x, 128 * m + k : 128 * m + k + 16, :].astype(F32)[half : half + 8]
                        odd = src[x, 128 * m + 64 + k : 128 * m + 64 + k + 16, :].astype(F32)[half : half + 8]
                    cols = slice(128 * m, 128 * m + 128)
                    grad_in[at, cols] = jnp.where(left, even, pltpu.roll(odd, 64, 1))
                    grad_out[at, cols] = jnp.where(left, pltpu.roll(even, 64, 1), odd)
            for j in range(4):
                rows, cols = slice(16 * q, 16 * q + 16), slice(128 * j, 128 * j + 128)
                node_grad[rows, cols] = src[x, 512 + 16 * j : 528 + 16 * j, :]
                node_out[rows, cols] = src[x, 576 + 16 * j : 592 + 16 * j, :]

    @pl.when(c_ref[0] == 0)
    def _():
        lay(mine, 0)
        lay(other, 1)

    @pl.when(c_ref[0] == 1)
    def _():
        lay(other, 0)
        lay(mine, 1)


def shards(nodes, adjacency, gain, w_in, w_out, cotangent):
    p = lax.axis_index("rep")
    own = lambda a: lax.dynamic_slice_in_dim(a, p * 16, 16, 0)
    at = p.reshape(1)
    core = (p % 2).reshape(1)
    moved = lax.ppermute(jnp.stack([own(nodes), own(cotangent)]), ALL, OUT)

    part = dot(adjacency, nodes, 0, 0).astype(BF).reshape(8, 128, 512)
    part = jnp.sum(trade(part, ALONG_V).astype(F32), axis=0).reshape(8, 16, 512)
    got = trade(part, ALONG_U)

    out, send, gain_part = call(
        update,
        [((16, 512), BF), ((8, 16, 1664), BF), ((8, 128), F32)],
        got, gain.reshape(1, 512), w_in, w_out, moved,
        scalar=core,
    )
    out = lax.ppermute(out, ALL, BACK)
    (send,) = call(forward_on, [((8, 128, 768), BF)], trade(send, ALONG_U))
    (send,) = call(
        back_and_tile, [((8, 80, 128), F32)], adjacency, trade(send, ALONG_V), gain_part, scalar=core
    )
    grad, send = call(
        add_up, [((64, 128), BF), ((8, 16, 128), BF)],
        lax.all_to_all(send, "rep", 0, 0), cotangent,
        scalar=at,
    )
    table = trade(send, ALONG_U)
    table = trade(jnp.broadcast_to(table, (8, 8, 16, 128)), ALONG_V).reshape(64, 16, 128)
    send, grad_gain = call(pack, [((4, 640, 128), BF), ((8, 128), F32)], table, grad, out)
    mine = trade(send, ALONG_X)
    other = lax.ppermute(mine, ALL, CORE)
    grad_in, grad_out, node_grad, node_out = call(
        unpack,
        [((512, 512), F32), ((512, 512), F32), ((128, 512), BF), ((128, 512), BF)],
        mine, other,
        scalar=core,
    )
    return (node_out, node_grad, grad_in, grad_out, grad_gain[:4].reshape(512))


def solution(mesh):
    return jax.shard_map(
        shards,
        mesh=mesh,
        in_specs=(P("rows", None), P("rows", "rep"), P(), P(), P(), P("rows", None)),
        out_specs=(P("rows", None), P("rows", None), P(), P(), P()),
        check_vma=False,
    )
```

```python
import jax
import jax.numpy as jnp
from jax import lax
from jax.experimental import pallas as pl
from jax.experimental.pallas import tpu as pltpu
from jax.sharding import PartitionSpec as P


BF = jnp.bfloat16
F32 = jnp.float32
ALL = ("rows", "rep")


def place(u, v, p):
    z, y = (v, u) if p % 2 == 0 else (u, v)
    return (8 * z + y) * 8 + p


E8 = range(8)
ALONG_U = [[place(u, v, p) for u in E8] for v in E8 for p in E8]
ALONG_V = [[place(u, v, p) for v in E8] for u in E8 for p in E8]
ALONG_X = [[r * 8 + 2 * x + c for x in range(4)] for r in range(64) for c in range(2)]
OUT = [((8 * z + y) * 8 + t, place(t, y, z)) for z in E8 for y in E8 for t in E8]
BACK = [(b, a) for a, b in OUT]
CORE = [(i, i ^ 1) for i in range(512)]


def dot(a, b, ca, cb):
    return lax.dot_general(a, b, (((ca,), (cb,)), ((), ())), preferred_element_type=F32)


def trade(x, groups):
    return lax.all_to_all(x, ALL, 0, 0, axis_index_groups=groups)


def call(body, outs, *args, scalar=None, scratch=()):
    specs = [pl.BlockSpec(memory_space=pltpu.VMEM)] * len(args)
    if scalar is not None:
        args = (scalar,) + args
        specs = [pl.BlockSpec(memory_space=pltpu.SMEM)] + specs
    return pl.pallas_call(
        body,
        out_shape=[jax.ShapeDtypeStruct(s, d) for s, d in outs],
        in_specs=specs,
        out_specs=[pl.BlockSpec(memory_space=pltpu.VMEM)] * len(outs),
        scratch_shapes=list(scratch),
        compiler_params=pltpu.CompilerParams(vmem_limit_bytes=40 * 1024 * 1024),
    )(*args)


def left_half():
    return lax.broadcasted_iota(jnp.int32, (1, 128), 1) < 64


def total_of(got):
    total = got[0].astype(F32)
    for i in range(1, 8):
        total = total + got[i].astype(F32)
    return total


def sum_and_copy(got, send):
    total = total_of(got).astype(BF)
    for u in E8:
        send[u] = total


def update(at_ref, got, gain_ref, w_in_ref, w_out_ref, cot_ref, out_ref, send, gain_part, rows, columns):
    summed = total_of(got)
    gain = gain_ref[...]
    w_in, w_out = w_in_ref[...], w_out_ref[...]
    cot = cot_ref[...]
    scale = lax.rsqrt(jnp.mean(summed * summed, axis=-1, keepdims=True) + 1e-05)
    normed = summed * scale
    lifted = (normed * gain).astype(BF)
    pre = dot(lifted, w_in, 1, 0)
    grad_hidden = dot(cot, w_out, 1, 1)
    sigma = jax.nn.sigmoid(pre)
    hidden = (pre * sigma).astype(BF)
    grad_pre = (grad_hidden * sigma * (1.0 + pre * (1.0 - sigma))).astype(BF)
    grad_lifted = dot(grad_pre, w_in, 1, 1)
    out_ref[...] = dot(hidden, w_out, 1, 0).astype(BF)
    gain_row = jnp.sum(grad_lifted * normed, axis=0, keepdims=True) * 0.125
    gain_part[...] = jnp.zeros_like(gain_part)
    for j in range(4):
        gain_part[j : j + 1, :] = gain_row[:, 128 * j : 128 * j + 128]
    grad_normed = grad_lifted * gain
    grad_summed = (
        scale * (grad_normed - normed * jnp.mean(grad_normed * normed, axis=-1, keepdims=True))
    ).astype(BF)
    for v in E8:
        send[v, 0:128, :] = grad_summed
    left = left_half()

    def pairs(a, b, ref):
        a, b = a.astype(F32), b.astype(F32)
        for m in range(4):
            one, two = a[:, 128 * m : 128 * m + 128], b[:, 128 * m : 128 * m + 128]
            ref[2 * m] = jnp.where(left, one, pltpu.roll(two, 64, 1)).astype(BF)
            ref[2 * m + 1] = jnp.where(left, pltpu.roll(one, 64, 1), two).astype(BF)

    pairs(lifted, hidden, rows)
    pairs(grad_pre, cot, columns)
    first, u = at_ref[0] == 0, at_ref[1]
    for k in E8:
        tile = dot(rows[jnp.where(first, k, u)], columns[jnp.where(first, u, k)], 0, 0)
        tile = jnp.where(left, tile[0:64], tile[64:128])
        high = tile.astype(BF)
        low = (tile - high.astype(F32)).astype(BF)
        for j in range(4):
            at = slice(128 * j, 128 * j + 128)
            send[k, 128:144, at] = high[16 * j : 16 * j + 16]
            send[k, 144:160, at] = low[16 * j : 16 * j + 16]


def back_and_tile(adjacency, got, gain_part, send):
    field = got[:, 0:128, :].reshape(1024, 512)
    back = dot(adjacency[...], field, 1, 0)
    for q in E8:
        for j in range(4):
            send[q, 16 * j : 16 * j + 16, :] = back[16 * q : 16 * q + 16, 128 * j : 128 * j + 128]
    tile = jnp.zeros((16, 512), F32)
    for v in E8:
        tile = tile + (got[v, 128:144, :].astype(F32) + got[v, 144:160, :].astype(F32))
    part = gain_part[...]
    for q in E8:
        at = slice(128 * (q // 2), 128 * (q // 2) + 128)
        send[q, 64:72, :] = tile[8 * (q % 2) : 8 * (q % 2) + 8, at]
        send[q, 72:80, :] = part


def add_up(p_ref, got, cotangent, grad, send):
    total = total_of(got)
    own = cotangent[pl.ds(pl.multiple_of(p_ref[0] * 16, 16), 16), :].astype(F32)
    for j in range(4):
        grad[16 * j : 16 * j + 16, :] = (
            own[:, 128 * j : 128 * j + 128] + total[16 * j : 16 * j + 16]
        ).astype(BF)
    block = total[64:80].astype(BF)
    for r in range(64):
        send[r] = block


def pack(got, grad, send, gain):
    total = jnp.zeros((8, 128), F32)
    for i in range(32):
        one, two = got[2 * i].astype(F32), got[2 * i + 1].astype(F32)
        total = total + one[8:16] + two[8:16]
        both = jnp.concatenate([one[0:8], two[0:8]], axis=0).astype(BF)
        for x in range(4):
            send[x, 16 * i : 16 * i + 16, :] = both
    gain[...] = total
    grad = grad[...]
    for x in range(4):
        send[x, 512:576, :] = grad


def unpack(c_ref, mine, other, nodes, change, grad_in, grad_out, node_grad, node_out):
    node_out[...] = (nodes[...].astype(F32) + change[...].astype(F32)).astype(BF)
    left = left_half()

    def lay(src, c):
        for x in range(4):
            q = 2 * x + c
            for z in E8:
                at = slice(64 * z + 8 * q, 64 * z + 8 * q + 8)
                for m in range(4):
                    both = src[x, 64 * z + 16 * m : 64 * z + 16 * m + 16, :].astype(F32)
                    even, odd = both[0:8], both[8:16]
                    cols = slice(128 * m, 128 * m + 128)
                    grad_in[at, cols] = jnp.where(left, even, pltpu.roll(odd, 64, 1))
                    grad_out[at, cols] = jnp.where(left, pltpu.roll(even, 64, 1), odd)
            for j in range(4):
                rows, cols = slice(16 * q, 16 * q + 16), slice(128 * j, 128 * j + 128)
                node_grad[rows, cols] = src[x, 512 + 16 * j : 528 + 16 * j, :]

    @pl.when(c_ref[0] == 0)
    def _():
        lay(mine, 0)
        lay(other, 1)

    @pl.when(c_ref[0] == 1)
    def _():
        lay(other, 0)
        lay(mine, 1)


def shards(nodes, adjacency, gain, w_in, w_out, cotangent):
    r, p = lax.axis_index("rows"), lax.axis_index("rep")
    core = p % 2
    u = jnp.where(core == 0, r % 8, r // 8)
    cot = lax.ppermute(cotangent, ALL, OUT)

    part = dot(adjacency, nodes, 0, 0).astype(BF).reshape(8, 128, 512)
    (part,) = call(sum_and_copy, [((8, 128, 512), BF)], trade(part, ALONG_V))
    got = trade(part, ALONG_U)

    change, send, gain_part = call(
        update,
        [((128, 512), BF), ((8, 160, 512), BF), ((8, 128), F32)],
        got, gain.reshape(1, 512), w_in, w_out, cot,
        scalar=jnp.stack([core, u]),
        scratch=[pltpu.VMEM((8, 128, 128), BF)] * 2,
    )
    change = lax.ppermute(change, ALL, BACK)
    (send,) = call(back_and_tile, [((8, 80, 128), F32)], adjacency, trade(send, ALONG_V), gain_part)
    grad, send = call(
        add_up, [((64, 128), BF), ((64, 16, 128), BF)],
        lax.all_to_all(send, "rep", 0, 0), cotangent,
        scalar=p.reshape(1),
    )
    table = lax.all_to_all(send, "rows", 0, 0)
    send, grad_gain = call(pack, [((4, 576, 128), BF), ((8, 128), F32)], table, grad)
    mine = trade(send, ALONG_X)
    other = lax.ppermute(mine, ALL, CORE)
    grad_in, grad_out, node_grad, node_out = call(
        unpack,
        [((512, 512), F32), ((512, 512), F32), ((128, 512), BF), ((128, 512), BF)],
        mine, other, nodes, change,
        scalar=core.reshape(1),
    )
    return (node_out, node_grad, grad_in, grad_out, grad_gain[:4].reshape(512))


def solution(mesh):
    return jax.shard_map(
        shards,
        mesh=mesh,
        in_specs=(P("rows", None), P("rows", "rep"), P(), P(), P(), P("rows", None)),
        out_specs=(P("rows", None), P("rows", None), P(), P(), P()),
        check_vma=False,
    )
```

```python
import jax
import jax.numpy as jnp
from jax import lax
from jax.experimental import pallas as pl
from jax.experimental.pallas import tpu as pltpu
from jax.sharding import PartitionSpec as P


BF = jnp.bfloat16
F32 = jnp.float32
ALL = ("rows", "rep")


def place(u, v, p):
    z, y = (v, u) if p % 2 == 0 else (u, v)
    return (8 * z + y) * 8 + p


E8 = range(8)
ALONG_U = [[place(u, v, p) for u in E8] for v in E8 for p in E8]
ALONG_V = [[place(u, v, p) for v in E8] for u in E8 for p in E8]
ALONG_X = [[r * 8 + 2 * x + c for x in range(4)] for r in range(64) for c in range(2)]
OUT = [((8 * z + y) * 8 + t, place(t, y, z)) for z in E8 for y in E8 for t in E8]
BACK = [(b, a) for a, b in OUT]
CORE = [(i, i ^ 1) for i in range(512)]


def dot(a, b, ca, cb):
    return lax.dot_general(a, b, (((ca,), (cb,)), ((), ())), preferred_element_type=F32)


def trade(x, groups):
    return lax.all_to_all(x, ALL, 0, 0, axis_index_groups=groups)


def call(body, outs, *args, scalar=None, scratch=()):
    specs = [pl.BlockSpec(memory_space=pltpu.VMEM)] * len(args)
    if scalar is not None:
        args = (scalar,) + args
        specs = [pl.BlockSpec(memory_space=pltpu.SMEM)] + specs
    return pl.pallas_call(
        body,
        out_shape=[jax.ShapeDtypeStruct(s, d) for s, d in outs],
        in_specs=specs,
        out_specs=[pl.BlockSpec(memory_space=pltpu.VMEM)] * len(outs),
        scratch_shapes=list(scratch),
        compiler_params=pltpu.CompilerParams(vmem_limit_bytes=40 * 1024 * 1024),
    )(*args)


def left_half():
    return lax.broadcasted_iota(jnp.int32, (1, 128), 1) < 64


def total_of(got):
    total = got[0].astype(F32)
    for i in range(1, 8):
        total = total + got[i].astype(F32)
    return total


def sum_and_copy(got, cot, send):
    total, piece = total_of(got).astype(BF), cot[...]
    for u in E8:
        send[u, 0:128, :] = total
        send[u, 128:144, :] = piece


def update(at_ref, got, gain_ref, w_in_ref, w_out_ref, out_ref, send, gain_part, change, rows, columns):
    summed = got[0, 0:128, :].astype(F32)
    for i in range(1, 8):
        summed = summed + got[i, 0:128, :].astype(F32)
    gain = gain_ref[...]
    w_in, w_out = w_in_ref[...], w_out_ref[...]
    cot = got[:, 128:144, :].reshape(128, 512)
    scale = lax.rsqrt(jnp.mean(summed * summed, axis=-1, keepdims=True) + 1e-05)
    normed = summed * scale
    lifted = (normed * gain).astype(BF)
    pre = dot(lifted, w_in, 1, 0)
    grad_hidden = dot(cot, w_out, 1, 1)
    sigma = jax.nn.sigmoid(pre)
    hidden = (pre * sigma).astype(BF)
    grad_pre = (grad_hidden * sigma * (1.0 + pre * (1.0 - sigma))).astype(BF)
    grad_lifted = dot(grad_pre, w_in, 1, 1)
    change[...] = dot(hidden, w_out, 1, 0).astype(BF)
    out_ref[...] = change[pl.ds(pl.multiple_of(at_ref[1] * 16, 16), 16), :]
    gain_row = jnp.sum(grad_lifted * normed, axis=0, keepdims=True) * 0.125
    gain_part[...] = jnp.zeros_like(gain_part)
    for j in range(4):
        gain_part[j : j + 1, :] = gain_row[:, 128 * j : 128 * j + 128]
    grad_normed = grad_lifted * gain
    grad_summed = (
        scale * (grad_normed - normed * jnp.mean(grad_normed * normed, axis=-1, keepdims=True))
    ).astype(BF)
    for v in E8:
        send[v, 0:128, :] = grad_summed
    left = left_half()

    def pairs(a, b, ref):
        a, b = a.astype(F32), b.astype(F32)
        for m in range(4):
            one, two = a[:, 128 * m : 128 * m + 128], b[:, 128 * m : 128 * m + 128]
            ref[2 * m] = jnp.where(left, one, pltpu.roll(two, 64, 1)).astype(BF)
            ref[2 * m + 1] = jnp.where(left, pltpu.roll(one, 64, 1), two).astype(BF)

    pairs(lifted, hidden, rows)
    pairs(grad_pre, cot, columns)
    first, u = at_ref[0] == 0, at_ref[1]
    for k in E8:
        tile = dot(rows[jnp.where(first, k, u)], columns[jnp.where(first, u, k)], 0, 0)
        tile = jnp.where(left, tile[0:64], tile[64:128])
        high = tile.astype(BF)
        low = (tile - high.astype(F32)).astype(BF)
        for j in range(4):
            at = slice(128 * j, 128 * j + 128)
            send[k, 128:144, at] = high[16 * j : 16 * j + 16]
            send[k, 144:160, at] = low[16 * j : 16 * j + 16]


def back_and_tile(adjacency, got, gain_part, send):
    field = got[:, 0:128, :].reshape(1024, 512)
    back = dot(adjacency[...], field, 1, 0)
    for q in E8:
        for j in range(4):
            send[q, 16 * j : 16 * j + 16, :] = back[16 * q : 16 * q + 16, 128 * j : 128 * j + 128]
    tile = jnp.zeros((16, 512), F32)
    for v in E8:
        tile = tile + (got[v, 128:144, :].astype(F32) + got[v, 144:160, :].astype(F32))
    part = gain_part[...]
    for q in E8:
        at = slice(128 * (q // 2), 128 * (q // 2) + 128)
        send[q, 64:72, :] = tile[8 * (q % 2) : 8 * (q % 2) + 8, at]
        send[q, 72:80, :] = part


def add_up(p_ref, got, cotangent, grad, send):
    total = total_of(got)
    own = cotangent[pl.ds(pl.multiple_of(p_ref[0] * 16, 16), 16), :].astype(F32)
    for j in range(4):
        grad[16 * j : 16 * j + 16, :] = (
            own[:, 128 * j : 128 * j + 128] + total[16 * j : 16 * j + 16]
        ).astype(BF)
    block = total[64:80].astype(BF)
    for r in range(64):
        send[r] = block


def pack(got, grad, change, send, gain):
    total = jnp.zeros((8, 128), F32)
    for i in range(32):
        one, two = got[2 * i].astype(F32), got[2 * i + 1].astype(F32)
        total = total + one[8:16] + two[8:16]
        both = jnp.concatenate([one[0:8], two[0:8]], axis=0).astype(BF)
        for x in range(4):
            send[x, 16 * i : 16 * i + 16, :] = both
    gain[...] = total
    grad = grad[...]
    for x in range(4):
        send[x, 512:576, :] = grad
        for j in range(4):
            send[x, 576 + 16 * j : 592 + 16 * j, :] = change[:, 128 * j : 128 * j + 128]


def unpack(c_ref, mine, other, nodes, grad_in, grad_out, node_grad, node_out):
    left = left_half()

    def lay(src, c):
        for x in range(4):
            q = 2 * x + c
            for z in E8:
                at = slice(64 * z + 8 * q, 64 * z + 8 * q + 8)
                for m in range(4):
                    both = src[x, 64 * z + 16 * m : 64 * z + 16 * m + 16, :].astype(F32)
                    even, odd = both[0:8], both[8:16]
                    cols = slice(128 * m, 128 * m + 128)
                    grad_in[at, cols] = jnp.where(left, even, pltpu.roll(odd, 64, 1))
                    grad_out[at, cols] = jnp.where(left, pltpu.roll(even, 64, 1), odd)
            for j in range(4):
                rows, cols = slice(16 * q, 16 * q + 16), slice(128 * j, 128 * j + 128)
                node_grad[rows, cols] = src[x, 512 + 16 * j : 528 + 16 * j, :]
                change = src[x, 576 + 16 * j : 592 + 16 * j, :].astype(F32)
                node_out[rows, cols] = (nodes[rows, cols].astype(F32) + change).astype(BF)

    @pl.when(c_ref[0] == 0)
    def _():
        lay(mine, 0)
        lay(other, 1)

    @pl.when(c_ref[0] == 1)
    def _():
        lay(other, 0)
        lay(mine, 1)


def shards(nodes, adjacency, gain, w_in, w_out, cotangent):
    r, p = lax.axis_index("rows"), lax.axis_index("rep")
    core = p % 2
    u = jnp.where(core == 0, r % 8, r // 8)
    cot = lax.ppermute(lax.dynamic_slice_in_dim(cotangent, p * 16, 16, 0), ALL, OUT)

    part = dot(adjacency, nodes, 0, 0).astype(BF).reshape(8, 128, 512)
    (part,) = call(sum_and_copy, [((8, 144, 512), BF)], trade(part, ALONG_V), cot)
    got = trade(part, ALONG_U)

    change, send, gain_part = call(
        update,
        [((16, 512), BF), ((8, 160, 512), BF), ((8, 128), F32)],
        got, gain.reshape(1, 512), w_in, w_out,
        scalar=jnp.stack([core, u]),
        scratch=[pltpu.VMEM((128, 512), BF)] + [pltpu.VMEM((8, 128, 128), BF)] * 2,
    )
    change = lax.ppermute(change, ALL, BACK)
    (send,) = call(back_and_tile, [((8, 80, 128), F32)], adjacency, trade(send, ALONG_V), gain_part)
    grad, send = call(
        add_up, [((64, 128), BF), ((64, 16, 128), BF)],
        lax.all_to_all(send, "rep", 0, 0), cotangent,
        scalar=p.reshape(1),
    )
    table = lax.all_to_all(send, "rows", 0, 0)
    send, grad_gain = call(pack, [((4, 640, 128), BF), ((8, 128), F32)], table, grad, change)
    mine = trade(send, ALONG_X)
    other = lax.ppermute(mine, ALL, CORE)
    grad_in, grad_out, node_grad, node_out = call(
        unpack,
        [((512, 512), F32), ((512, 512), F32), ((128, 512), BF), ((128, 512), BF)],
        mine, other, nodes,
        scalar=core.reshape(1),
    )
    return (node_out, node_grad, grad_in, grad_out, grad_gain[:4].reshape(512))


def solution(mesh):
    return jax.shard_map(
        shards,
        mesh=mesh,
        in_specs=(P("rows", None), P("rows", "rep"), P(), P(), P(), P("rows", None)),
        out_specs=(P("rows", None), P("rows", None), P(), P(), P()),
        check_vma=False,
    )
```

```python
import jax
import jax.numpy as jnp
from jax import lax
from jax.experimental import pallas as pl
from jax.experimental.pallas import tpu as pltpu
from jax.sharding import PartitionSpec as P


BF = jnp.bfloat16
F32 = jnp.float32
ALL = ("rows", "rep")


def place(k, e, a, p):
    z, y = (k, 2 * a + e) if p % 2 == 0 else (2 * a + e, k)
    return (8 * z + y) * 8 + p


E8 = range(8)
WIDE = [[place(k, e, a, p) for k in E8 for e in range(2)] for a in range(4) for p in E8]
NARROW = [[place(k, e, a, p) for a in range(4)] for k in E8 for e in range(2) for p in E8]
ALONG_X = [[r * 8 + 2 * x + c for x in range(4)] for r in range(64) for c in range(2)]
OUT = [((8 * z + y) * 8 + t, place(y, t // 4, t % 4, z)) for z in E8 for y in E8 for t in E8]
BACK = [(b, a) for a, b in OUT]
CORE = [(i, i ^ 1) for i in range(512)]


def dot(a, b, ca, cb):
    return lax.dot_general(a, b, (((ca,), (cb,)), ((), ())), preferred_element_type=F32)


def trade(x, groups):
    return lax.all_to_all(x, ALL, 0, 0, axis_index_groups=groups)


def call(body, outs, *args, scalar=None, scratch=()):
    specs = [pl.BlockSpec(memory_space=pltpu.VMEM)] * len(args)
    if scalar is not None:
        args = (scalar,) + args
        specs = [pl.BlockSpec(memory_space=pltpu.SMEM)] + specs
    return pl.pallas_call(
        body,
        out_shape=[jax.ShapeDtypeStruct(s, d) for s, d in outs],
        in_specs=specs,
        out_specs=[pl.BlockSpec(memory_space=pltpu.VMEM)] * len(outs),
        scratch_shapes=list(scratch),
        compiler_params=pltpu.CompilerParams(vmem_limit_bytes=40 * 1024 * 1024),
    )(*args)


def left_half():
    return lax.broadcasted_iota(jnp.int32, (1, 128), 1) < 64


def total_of(got):
    total = got[0].astype(F32)
    for i in range(1, got.shape[0]):
        total = total + got[i].astype(F32)
    return total


def sum_and_copy(got, cot, send):
    total, piece = total_of(got), cot[...]
    high = total.astype(BF)
    low = (total - high.astype(F32)).astype(BF)
    for a in range(4):
        send[a, 0:64, :] = high
        send[a, 64:128, :] = low
        send[a, 128:144, :] = piece


def update(at_ref, got, gain_ref, w_in_ref, w_out_ref, out_ref, send, gain_part, change, rows, columns):
    summed = got[0, 0:64, :].astype(F32) + got[0, 64:128, :].astype(F32)
    for i in range(1, 4):
        summed = summed + (got[i, 0:64, :].astype(F32) + got[i, 64:128, :].astype(F32))
    gain = gain_ref[...]
    w_in, w_out = w_in_ref[...], w_out_ref[...]
    cot = got[:, 128:144, :].reshape(64, 512)
    scale = lax.rsqrt(jnp.mean(summed * summed, axis=-1, keepdims=True) + 1e-05)
    normed = summed * scale
    lifted = (normed * gain).astype(BF)
    pre = dot(lifted, w_in, 1, 0)
    grad_hidden = dot(cot, w_out, 1, 1)
    sigma = jax.nn.sigmoid(pre)
    hidden = (pre * sigma).astype(BF)
    grad_pre = (grad_hidden * sigma * (1.0 + pre * (1.0 - sigma))).astype(BF)
    grad_lifted = dot(grad_pre, w_in, 1, 1)
    change[...] = dot(hidden, w_out, 1, 0).astype(BF)
    out_ref[...] = change[pl.ds(pl.multiple_of(at_ref[1] * 16, 16), 16), :]
    gain_row = jnp.sum(grad_lifted * normed, axis=0, keepdims=True) * 0.25
    gain_part[...] = jnp.zeros_like(gain_part)
    for j in range(4):
        gain_part[j : j + 1, :] = gain_row[:, 128 * j : 128 * j + 128]
    grad_normed = grad_lifted * gain
    grad_summed = (
        scale * (grad_normed - normed * jnp.mean(grad_normed * normed, axis=-1, keepdims=True))
    ).astype(BF)
    for b in range(16):
        send[b, 0:64, :] = grad_summed
    left = left_half()

    def pairs(a, b, ref):
        a, b = a.astype(F32), b.astype(F32)
        for m in range(4):
            one, two = a[:, 128 * m : 128 * m + 128], b[:, 128 * m : 128 * m + 128]
            ref[2 * m] = jnp.where(left, one, pltpu.roll(two, 64, 1)).astype(BF)
            ref[2 * m + 1] = jnp.where(left, pltpu.roll(one, 64, 1), two).astype(BF)

    pairs(lifted, hidden, rows)
    pairs(grad_pre, cot, columns)
    first, a = at_ref[0] == 0, at_ref[1]
    for k in E8:
        for e in range(2):
            other = 2 * a + e
            tile = dot(rows[jnp.where(first, k, other)], columns[jnp.where(first, other, k)], 0, 0)
            tile = jnp.where(left, tile[0:64], tile[64:128]).astype(BF)
            for j in range(4):
                send[2 * k + e, 64:80, 128 * j : 128 * j + 128] = tile[16 * j : 16 * j + 16]


def back_and_tile(adjacency, got, gain_part, send):
    field = got[:, 0:64, :].reshape(1024, 512)
    back = dot(adjacency[...], field, 1, 0)
    for q in E8:
        for j in range(4):
            send[q, 16 * j : 16 * j + 16, :] = back[16 * q : 16 * q + 16, 128 * j : 128 * j + 128]
    tile = jnp.zeros((16, 512), F32)
    for b in range(16):
        tile = tile + got[b, 64:80, :].astype(F32)
    part = gain_part[...]
    for q in E8:
        at = slice(128 * (q // 2), 128 * (q // 2) + 128)
        send[q, 64:72, :] = tile[8 * (q % 2) : 8 * (q % 2) + 8, at]
        send[q, 72:80, :] = part


def add_up(p_ref, got, cotangent, grad, send):
    total = total_of(got)
    own = cotangent[pl.ds(pl.multiple_of(p_ref[0] * 16, 16), 16), :].astype(F32)
    for j in range(4):
        grad[16 * j : 16 * j + 16, :] = (
            own[:, 128 * j : 128 * j + 128] + total[16 * j : 16 * j + 16]
        ).astype(BF)
    block = total[64:80].astype(BF)
    for r in range(64):
        send[r] = block


def pack(got, grad, change, send, gain):
    total = jnp.zeros((8, 128), F32)
    for i in range(32):
        one, two = got[2 * i].astype(F32), got[2 * i + 1].astype(F32)
        total = total + one[8:16] + two[8:16]
        both = jnp.concatenate([one[0:8], two[0:8]], axis=0).astype(BF)
        for x in range(4):
            send[x, 16 * i : 16 * i + 16, :] = both
    gain[...] = total
    grad = grad[...]
    for x in range(4):
        send[x, 512:576, :] = grad
        for j in range(4):
            send[x, 576 + 16 * j : 592 + 16 * j, :] = change[:, 128 * j : 128 * j + 128]


def unpack(c_ref, mine, other, nodes, grad_in, grad_out, node_grad, node_out):
    left = left_half()

    def lay(src, c):
        for x in range(4):
            q = 2 * x + c
            for z in E8:
                at = slice(64 * z + 8 * q, 64 * z + 8 * q + 8)
                for m in range(4):
                    both = src[x, 64 * z + 16 * m : 64 * z + 16 * m + 16, :].astype(F32)
                    even, odd = both[0:8], both[8:16]
                    cols = slice(128 * m, 128 * m + 128)
                    grad_in[at, cols] = jnp.where(left, even, pltpu.roll(odd, 64, 1))
                    grad_out[at, cols] = jnp.where(left, pltpu.roll(even, 64, 1), odd)
            for j in range(4):
                rows, cols = slice(16 * q, 16 * q + 16), slice(128 * j, 128 * j + 128)
                node_grad[rows, cols] = src[x, 512 + 16 * j : 528 + 16 * j, :]
                change = src[x, 576 + 16 * j : 592 + 16 * j, :].astype(F32)
                node_out[rows, cols] = (nodes[rows, cols].astype(F32) + change).astype(BF)

    @pl.when(c_ref[0] == 0)
    def _():
        lay(mine, 0)
        lay(other, 1)

    @pl.when(c_ref[0] == 1)
    def _():
        lay(other, 0)
        lay(mine, 1)


def shards(nodes, adjacency, gain, w_in, w_out, cotangent):
    r, p = lax.axis_index("rows"), lax.axis_index("rep")
    core = p % 2
    a = jnp.where(core == 0, r % 8, r // 8) // 2
    cot = lax.ppermute(lax.dynamic_slice_in_dim(cotangent, p * 16, 16, 0), ALL, OUT)

    part = dot(adjacency, nodes, 0, 0).astype(BF).reshape(16, 64, 512)
    (part,) = call(sum_and_copy, [((4, 144, 512), BF)], trade(part, WIDE), cot)
    got = trade(part, NARROW)

    change, send, gain_part = call(
        update,
        [((16, 512), BF), ((16, 80, 512), BF), ((8, 128), F32)],
        got, gain.reshape(1, 512), w_in, w_out,
        scalar=jnp.stack([core, a]),
        scratch=[pltpu.VMEM((64, 512), BF)] + [pltpu.VMEM((8, 64, 128), BF)] * 2,
    )
    change = lax.ppermute(change, ALL, BACK)
    (send,) = call(back_and_tile, [((8, 80, 128), F32)], adjacency, trade(send, WIDE), gain_part)
    grad, send = call(
        add_up, [((64, 128), BF), ((64, 16, 128), BF)],
        lax.all_to_all(send, "rep", 0, 0), cotangent,
        scalar=p.reshape(1),
    )
    table = lax.all_to_all(send, "rows", 0, 0)
    send, grad_gain = call(pack, [((4, 640, 128), BF), ((8, 128), F32)], table, grad, change)
    mine = trade(send, ALONG_X)
    other = lax.ppermute(mine, ALL, CORE)
    grad_in, grad_out, node_grad, node_out = call(
        unpack,
        [((512, 512), F32), ((512, 512), F32), ((128, 512), BF), ((128, 512), BF)],
        mine, other, nodes,
        scalar=core.reshape(1),
    )
    return (node_out, node_grad, grad_in, grad_out, grad_gain[:4].reshape(512))


def solution(mesh):
    return jax.shard_map(
        shards,
        mesh=mesh,
        in_specs=(P("rows", None), P("rows", "rep"), P(), P(), P(), P("rows", None)),
        out_specs=(P("rows", None), P("rows", None), P(), P(), P()),
        check_vma=False,
    )
```

```python
import jax
import jax.numpy as jnp
from jax import lax
from jax.experimental import pallas as pl
from jax.experimental.pallas import tpu as pltpu
from jax.sharding import PartitionSpec as P


BF = jnp.bfloat16
F32 = jnp.float32
ALL = ("rows", "rep")


def place(u, v, p):
    z, y = (v, u) if p % 2 == 0 else (u, v)
    return (8 * z + y) * 8 + p


E8 = range(8)
ALONG_U = [[place(u, v, p) for u in E8] for v in E8 for p in E8]
ALONG_V = [[place(u, v, p) for v in E8] for u in E8 for p in E8]
ALONG_X = [[r * 8 + 2 * x + c for x in range(4)] for r in range(64) for c in range(2)]
OUT = [((8 * z + y) * 8 + t, place(t, y, z)) for z in E8 for y in E8 for t in E8]
BACK = [(b, a) for a, b in OUT]
CORE = [(i, i ^ 1) for i in range(512)]


def dot(a, b, ca, cb):
    return lax.dot_general(a, b, (((ca,), (cb,)), ((), ())), preferred_element_type=F32)


def trade(x, groups):
    return lax.all_to_all(x, ALL, 0, 0, axis_index_groups=groups)


def call(body, outs, at, *args, scratch=()):
    return pl.pallas_call(
        body,
        out_shape=[jax.ShapeDtypeStruct(s, d) for s, d in outs],
        in_specs=[pl.BlockSpec(memory_space=pltpu.SMEM)] + [pl.BlockSpec(memory_space=pltpu.VMEM)] * len(args),
        out_specs=[pl.BlockSpec(memory_space=pltpu.VMEM)] * len(outs),
        scratch_shapes=list(scratch),
        compiler_params=pltpu.CompilerParams(vmem_limit_bytes=40 * 1024 * 1024),
    )(at, *args)


def left_half():
    return lax.broadcasted_iota(jnp.int32, (1, 128), 1) < 64


def total_of(got):
    total = got[0].astype(F32)
    for i in range(1, 8):
        total = total + got[i].astype(F32)
    return total


def sum_and_copy(at_ref, got, cot, send):
    total, piece = total_of(got).astype(BF), cot[...]
    for u in E8:
        send[u, 0:128, :] = total
        send[u, 128:144, :] = piece


def update(at_ref, got, gain_ref, w_in_ref, w_out_ref, out_ref, send, gain_part, change, rows, columns):
    summed = got[0, 0:128, :].astype(F32)
    for i in range(1, 8):
        summed = summed + got[i, 0:128, :].astype(F32)
    gain = gain_ref[...]
    w_in, w_out = w_in_ref[...], w_out_ref[...]
    cot = got[:, 128:144, :].reshape(128, 512)
    scale = lax.rsqrt(jnp.mean(summed * summed, axis=-1, keepdims=True) + 1e-05)
    normed = summed * scale
    lifted = (normed * gain).astype(BF)
    pre = dot(lifted, w_in, 1, 0)
    grad_hidden = dot(cot, w_out, 1, 1)
    sigma = jax.nn.sigmoid(pre)
    hidden = (pre * sigma).astype(BF)
    grad_pre = (grad_hidden * sigma * (1.0 + pre * (1.0 - sigma))).astype(BF)
    grad_lifted = dot(grad_pre, w_in, 1, 1)
    change[...] = dot(hidden, w_out, 1, 0).astype(BF)
    out_ref[...] = change[pl.ds(pl.multiple_of(at_ref[1] * 16, 16), 16), :]
    gain_row = jnp.sum(grad_lifted * normed, axis=0, keepdims=True) * 0.125
    gain_part[...] = jnp.zeros_like(gain_part)
    for j in range(4):
        gain_part[j : j + 1, :] = gain_row[:, 128 * j : 128 * j + 128]
    grad_normed = grad_lifted * gain
    grad_summed = (
        scale * (grad_normed - normed * jnp.mean(grad_normed * normed, axis=-1, keepdims=True))
    ).astype(BF)
    for v in E8:
        send[v, 0:128, :] = grad_summed
    left = left_half()

    def pairs(a, b, ref):
        a, b = a.astype(F32), b.astype(F32)
        for m in range(4):
            one, two = a[:, 128 * m : 128 * m + 128], b[:, 128 * m : 128 * m + 128]
            ref[2 * m] = jnp.where(left, one, pltpu.roll(two, 64, 1)).astype(BF)
            ref[2 * m + 1] = jnp.where(left, pltpu.roll(one, 64, 1), two).astype(BF)

    pairs(lifted, hidden, rows)
    pairs(grad_pre, cot, columns)
    first, u = at_ref[0] == 0, at_ref[1]
    for k in E8:
        tile = dot(rows[jnp.where(first, k, u)], columns[jnp.where(first, u, k)], 0, 0)
        tile = jnp.where(left, tile[0:64], tile[64:128])
        high = tile.astype(BF)
        low = (tile - high.astype(F32)).astype(BF)
        for j in range(4):
            at = slice(128 * j, 128 * j + 128)
            send[k, 128:144, at] = high[16 * j : 16 * j + 16]
            send[k, 144:160, at] = low[16 * j : 16 * j + 16]


def back_and_tile(at_ref, adjacency, got, gain_part, send):
    field = got[:, 0:128, :].reshape(1024, 512)
    back = dot(adjacency[...], field, 1, 0)
    for q in E8:
        for j in range(4):
            send[q, 16 * j : 16 * j + 16, :] = back[16 * q : 16 * q + 16, 128 * j : 128 * j + 128].astype(BF)
    tile = jnp.zeros((16, 512), F32)
    for v in E8:
        tile = tile + (got[v, 128:144, :].astype(F32) + got[v, 144:160, :].astype(F32))
    part = gain_part[...]
    for q in E8:
        at = slice(128 * (q // 2), 128 * (q // 2) + 128)
        exact = jnp.concatenate([tile[8 * (q % 2) : 8 * (q % 2) + 8, at], part], axis=0)
        high = exact.astype(BF)
        send[q, 64:80, :] = high
        send[q, 80:96, :] = (exact - high.astype(F32)).astype(BF)


def add_up(at_ref, got, cotangent, grad, send):
    total = total_of(got)
    own = cotangent[pl.ds(pl.multiple_of(at_ref[2] * 16, 16), 16), :].astype(F32)
    for j in range(4):
        grad[16 * j : 16 * j + 16, :] = (
            own[:, 128 * j : 128 * j + 128] + total[16 * j : 16 * j + 16]
        ).astype(BF)
    block = (total[64:80] + total[80:96]).astype(BF)
    for r in range(64):
        send[r] = block


def pack(at_ref, got, grad, change, send, gain):
    total = jnp.zeros((8, 128), F32)
    for i in range(32):
        one, two = got[2 * i].astype(F32), got[2 * i + 1].astype(F32)
        total = total + one[8:16] + two[8:16]
        both = jnp.concatenate([one[0:8], two[0:8]], axis=0).astype(BF)
        for x in range(4):
            send[x, 16 * i : 16 * i + 16, :] = both
    gain[...] = total
    grad = grad[...]
    for x in range(4):
        send[x, 512:576, :] = grad
        for j in range(4):
            send[x, 576 + 16 * j : 592 + 16 * j, :] = change[:, 128 * j : 128 * j + 128]


def unpack(at_ref, mine, other, nodes, grad_in, grad_out, node_grad, node_out):
    left = left_half()

    def lay(src, c):
        for x in range(4):
            q = 2 * x + c
            for z in E8:
                at = slice(64 * z + 8 * q, 64 * z + 8 * q + 8)
                for m in range(4):
                    both = src[x, 64 * z + 16 * m : 64 * z + 16 * m + 16, :].astype(F32)
                    even, odd = both[0:8], both[8:16]
                    cols = slice(128 * m, 128 * m + 128)
                    grad_in[at, cols] = jnp.where(left, even, pltpu.roll(odd, 64, 1))
                    grad_out[at, cols] = jnp.where(left, pltpu.roll(even, 64, 1), odd)
            for j in range(4):
                rows, cols = slice(16 * q, 16 * q + 16), slice(128 * j, 128 * j + 128)
                node_grad[rows, cols] = src[x, 512 + 16 * j : 528 + 16 * j, :]
                change = src[x, 576 + 16 * j : 592 + 16 * j, :].astype(F32)
                node_out[rows, cols] = (nodes[rows, cols].astype(F32) + change).astype(BF)

    @pl.when(at_ref[0] == 0)
    def _():
        lay(mine, 0)
        lay(other, 1)

    @pl.when(at_ref[0] == 1)
    def _():
        lay(other, 0)
        lay(mine, 1)


def shards(nodes, adjacency, gain, w_in, w_out, cotangent):
    r, p = lax.axis_index("rows"), lax.axis_index("rep")
    core = p & 1
    at = jnp.stack([core, jnp.where(core == 0, r & 7, r >> 3), p])
    cot = lax.ppermute(lax.dynamic_slice_in_dim(cotangent, p * 16, 16, 0), ALL, OUT)

    part = dot(adjacency, nodes, 0, 0).astype(BF).reshape(8, 128, 512)
    (part,) = call(sum_and_copy, [((8, 144, 512), BF)], at, trade(part, ALONG_V), cot)
    got = trade(part, ALONG_U)

    change, send, gain_part = call(
        update,
        [((16, 512), BF), ((8, 160, 512), BF), ((8, 128), F32)],
        at, got, gain.reshape(1, 512), w_in, w_out,
        scratch=[pltpu.VMEM((128, 512), BF)] + [pltpu.VMEM((8, 128, 128), BF)] * 2,
    )
    change = lax.ppermute(change, ALL, BACK)
    (send,) = call(back_and_tile, [((8, 96, 128), BF)], at, adjacency, trade(send, ALONG_V), gain_part)
    grad, send = call(
        add_up, [((64, 128), BF), ((64, 16, 128), BF)],
        at, lax.all_to_all(send, "rep", 0, 0), cotangent,
    )
    table = lax.all_to_all(send, "rows", 0, 0)
    send, grad_gain = call(pack, [((4, 640, 128), BF), ((8, 128), F32)], at, table, grad, change)
    mine = trade(send, ALONG_X)
    other = lax.ppermute(mine, ALL, CORE)
    grad_in, grad_out, node_grad, node_out = call(
        unpack,
        [((512, 512), F32), ((512, 512), F32), ((128, 512), BF), ((128, 512), BF)],
        at, mine, other, nodes,
    )
    return (node_out, node_grad, grad_in, grad_out, grad_gain[:4].reshape(512))


def solution(mesh):
    return jax.shard_map(
        shards,
        mesh=mesh,
        in_specs=(P("rows", None), P("rows", "rep"), P(), P(), P(), P("rows", None)),
        out_specs=(P("rows", None), P("rows", None), P(), P(), P()),
        check_vma=False,
    )
```

```python
import jax
import jax.numpy as jnp
from jax import lax
from jax.experimental import pallas as pl
from jax.experimental.pallas import tpu as pltpu
from jax.sharding import PartitionSpec as P


BF = jnp.bfloat16
F32 = jnp.float32
ALL = ("rows", "rep")


def place(u, v, p):
    z, y = (v, u) if p % 2 == 0 else (u, v)
    return (8 * z + y) * 8 + p


E8 = range(8)
ALONG_U = [[place(u, v, p) for u in E8] for v in E8 for p in E8]
ALONG_V = [[place(u, v, p) for v in E8] for u in E8 for p in E8]
OUT = [((8 * z + y) * 8 + t, place(t, y, z)) for z in E8 for y in E8 for t in E8]
BACK = [(b, a) for a, b in OUT]
CORE = [(i, i ^ 1) for i in range(512)]
SHIFT_X = [[(i, (i & ~7) | ((i + 2 * d) & 7)) for i in range(512)] for d in (1, 2, 3)]


def dot(a, b, ca, cb):
    return lax.dot_general(a, b, (((ca,), (cb,)), ((), ())), preferred_element_type=F32)


def trade(x, groups):
    return lax.all_to_all(x, ALL, 0, 0, axis_index_groups=groups)


def call(body, outs, *args, scratch=()):
    return pl.pallas_call(
        body,
        out_shape=[jax.ShapeDtypeStruct(s, d) for s, d in outs],
        in_specs=[pl.BlockSpec(memory_space=pltpu.VMEM)] * len(args),
        out_specs=[pl.BlockSpec(memory_space=pltpu.VMEM)] * len(outs),
        scratch_shapes=list(scratch),
        compiler_params=pltpu.CompilerParams(vmem_limit_bytes=40 * 1024 * 1024),
    )(*args)


def is_core_0():
    return (lax.axis_index("rep") & 1) == 0


def left_half():
    return lax.broadcasted_iota(jnp.int32, (1, 128), 1) < 64


def total_of(got):
    total = got[0].astype(F32)
    for i in range(1, 8):
        total = total + got[i].astype(F32)
    return total


def sum_and_copy(got, cot, send):
    total, piece = total_of(got).astype(BF), cot[...]
    for u in E8:
        send[u, 0:128, :] = total
        send[u, 128:144, :] = piece


def update(got, gain_ref, w_in_ref, w_out_ref, out_ref, send, change, rows, columns):
    summed = got[0, 0:128, :].astype(F32)
    for i in range(1, 8):
        summed = summed + got[i, 0:128, :].astype(F32)
    r = lax.axis_index("rows")
    first = is_core_0()
    u = jnp.where(first, r & 7, r >> 3)
    gain = gain_ref[...]
    w_in, w_out = w_in_ref[...], w_out_ref[...]
    cot = got[:, 128:144, :].reshape(128, 512)
    scale = lax.rsqrt(jnp.mean(summed * summed, axis=-1, keepdims=True) + 1e-05)
    normed = summed * scale
    lifted = (normed * gain).astype(BF)
    pre = dot(lifted, w_in, 1, 0)
    grad_hidden = dot(cot, w_out, 1, 1)
    sigma = jax.nn.sigmoid(pre)
    hidden = (pre * sigma).astype(BF)
    grad_pre = (grad_hidden * sigma * (1.0 + pre * (1.0 - sigma))).astype(BF)
    grad_lifted = dot(grad_pre, w_in, 1, 1)
    change[...] = dot(hidden, w_out, 1, 0).astype(BF)
    out_ref[...] = change[pl.ds(pl.multiple_of(u * 16, 16), 16), :]
    gain_row = jnp.sum(grad_lifted * normed, axis=0, keepdims=True)
    gain_high = gain_row.astype(BF).astype(F32)
    gain_rows = jnp.concatenate([gain_high, gain_row - gain_high, jnp.zeros((14, 512), F32)], axis=0).astype(BF)
    grad_normed = grad_lifted * gain
    grad_summed = (
        scale * (grad_normed - normed * jnp.mean(grad_normed * normed, axis=-1, keepdims=True))
    ).astype(BF)
    for v in E8:
        send[v, 0:128, :] = grad_summed
        send[v, 160:176, :] = gain_rows
    left = left_half()

    def pairs(a, b, ref):
        a, b = a.astype(F32), b.astype(F32)
        for m in range(4):
            one, two = a[:, 128 * m : 128 * m + 128], b[:, 128 * m : 128 * m + 128]
            ref[2 * m] = jnp.where(left, one, pltpu.roll(two, 64, 1)).astype(BF)
            ref[2 * m + 1] = jnp.where(left, pltpu.roll(one, 64, 1), two).astype(BF)

    pairs(lifted, hidden, rows)
    pairs(grad_pre, cot, columns)
    for k in E8:
        tile = dot(rows[jnp.where(first, k, u)], columns[jnp.where(first, u, k)], 0, 0)
        tile = jnp.where(left, tile[0:64], tile[64:128])
        high = tile.astype(BF)
        low = (tile - high.astype(F32)).astype(BF)
        for j in range(4):
            at = slice(128 * j, 128 * j + 128)
            send[k, 128:144, at] = high[16 * j : 16 * j + 16]
            send[k, 144:160, at] = low[16 * j : 16 * j + 16]


def back_and_tile(adjacency, got, nodes, change, send, out):
    own = nodes[pl.ds(pl.multiple_of(lax.axis_index("rep") * 16, 16), 16), :].astype(F32)
    final = (own + change[...].astype(F32)).astype(BF)
    for j in range(4):
        out[16 * j : 16 * j + 16, :] = final[:, 128 * j : 128 * j + 128]
    field = got[:, 0:128, :].reshape(1024, 512)
    back = dot(adjacency[...], field, 1, 0)
    for q in E8:
        for j in range(4):
            send[q, 16 * j : 16 * j + 16, :] = back[16 * q : 16 * q + 16, 128 * j : 128 * j + 128].astype(BF)
    exact = jnp.zeros((32, 512), F32)
    for v in E8:
        low = jnp.concatenate([got[v, 144:160, :], jnp.zeros((16, 512), BF)], axis=0)
        exact = exact + (jnp.concatenate([got[v, 128:144, :], got[v, 160:176, :]], axis=0).astype(F32) + low.astype(F32))
    gain = exact[16:17] + exact[17:18]
    gain = jnp.concatenate([gain[:, 128 * j : 128 * j + 128] for j in range(4)] + [jnp.zeros((4, 128), F32)], axis=0)
    high = exact[0:16].astype(BF)
    low = (exact[0:16] - high.astype(F32)).astype(BF)
    gain_high = gain.astype(BF).astype(F32)
    gain = jnp.concatenate([gain_high, gain - gain_high], axis=0).astype(BF)
    for q in E8:
        for i in range(2):
            j = 2 * (q % 2) + i
            send[q, 64 + 16 * i : 80 + 16 * i, :] = high[:, 128 * j : 128 * j + 128]
            send[q, 96 + 16 * i : 112 + 16 * i, :] = low[:, 128 * j : 128 * j + 128]
        send[q, 128:144, :] = gain


def add_up(got, cotangent, out, piece, send, gain):
    total = total_of(got)
    own = cotangent[pl.ds(pl.multiple_of(lax.axis_index("rep") * 16, 16), 16), :].astype(F32)
    for j in range(4):
        piece[16 * j : 16 * j + 16, :] = (
            own[:, 128 * j : 128 * j + 128] + total[16 * j : 16 * j + 16]
        ).astype(BF)
    piece[64:128, :] = out[...]
    block = (total[64:96] + total[96:128]).astype(BF)
    for r in range(64):
        send[r] = block
    gain[...] = total[128:136] + total[136:144]


def lay_rows(src, z, grad_in, grad_out):
    left = left_half()
    for m in range(4):
        even, odd = src[8 * z + 2 * m].astype(F32), src[8 * z + 2 * m + 1].astype(F32)
        cols = slice(128 * m, 128 * m + 128)
        grad_in[z, :, cols] = jnp.where(left, even, pltpu.roll(odd, 64, 1))
        grad_out[z, :, cols] = jnp.where(left, pltpu.roll(even, 64, 1), odd)


def lay(src, p0, p1, p2, p3, grad_in, grad_out, node_grad, node_out):
    for z in E8:
        lay_rows(src, z, grad_in, grad_out)
    p = lax.axis_index("rep")
    c = p & 1
    for d, pieces in enumerate((p0, p1, p2, p3)):
        for h in range(2):
            q = (((p >> 1) + 4 - d) & 3) * 2 + (c ^ h)
            rows = pl.ds(pl.multiple_of(16 * q, 16), 16)
            for j in range(4):
                cols = slice(128 * j, 128 * j + 128)
                node_grad[rows, cols] = pieces[h, 16 * j : 16 * j + 16, :]
                node_out[rows, cols] = pieces[h, 64 + 16 * j : 80 + 16 * j, :]


def lay_both(src, mine_in, mine_out, grad_in, grad_out, part_in, part_out, sems):
    c = lax.axis_index("rep") & 1
    copies = []

    def send(a, b, z, at):
        copies.append(pltpu.make_async_copy(a.at[z], b.at[z, at], sems.at[len(copies)]))
        copies[-1].start()

    for z in E8:
        send(mine_in, grad_in, z, c)
        send(mine_out, grad_out, z, c)
    for z in E8:
        lay_rows(src, z, part_in, part_out)
        send(part_in, grad_in, z, 1 - c)
        send(part_out, grad_out, z, 1 - c)
    for copy in copies:
        copy.wait()


def shards(nodes, adjacency, gain, w_in, w_out, cotangent):
    piece = lax.dynamic_slice_in_dim(cotangent, lax.axis_index("rep") * 16, 16, 0)
    cot = lax.ppermute(piece, ALL, OUT)

    part = dot(adjacency, nodes, 0, 0).astype(BF).reshape(8, 128, 512)
    (part,) = call(sum_and_copy, [((8, 144, 512), BF)], trade(part, ALONG_V), cot)
    got = trade(part, ALONG_U)

    change, send = call(
        update,
        [((16, 512), BF), ((8, 176, 512), BF)],
        got, gain.reshape(1, 512), w_in, w_out,
        scratch=[pltpu.VMEM((128, 512), BF)] + [pltpu.VMEM((8, 128, 128), BF)] * 2,
    )
    change = lax.ppermute(change, ALL, BACK)
    send, out = call(
        back_and_tile, [((8, 144, 128), BF), ((64, 128), BF)],
        adjacency, trade(send, ALONG_V), nodes, change,
    )
    piece, send, grad_gain = call(
        add_up, [((128, 128), BF), ((64, 32, 128), BF), ((8, 128), F32)],
        lax.all_to_all(send, "rep", 0, 0), cotangent, out,
    )
    mine = lax.all_to_all(send, "rows", 0, 0)
    pieces = jnp.stack([piece, lax.ppermute(piece, ALL, CORE)])
    pieces = [pieces] + [lax.ppermute(pieces, ALL, perm) for perm in SHIFT_X]
    mine, pieces = lax.optimization_barrier((mine, pieces))
    other = lax.ppermute(mine, ALL, CORE)
    half = ((8, 32, 512), F32)
    mine_in, mine_out, node_grad, node_out = call(
        lay, [half, half, ((128, 512), BF), ((128, 512), BF)], mine, *pieces
    )
    whole = jax.ShapeDtypeStruct((8, 2, 32, 512), F32)
    vmem = pl.BlockSpec(memory_space=pltpu.VMEM)
    grad_in, grad_out = pl.pallas_call(
        lay_both,
        out_shape=[whole, whole],
        in_specs=[vmem] * 3,
        out_specs=[pl.BlockSpec(memory_space=pl.ANY)] * 2,
        scratch_shapes=[pltpu.VMEM(*half)] * 2 + [pltpu.SemaphoreType.DMA((32,))],
        compiler_params=pltpu.CompilerParams(vmem_limit_bytes=40 * 1024 * 1024),
    )(other, mine_in, mine_out)
    return (node_out, node_grad, grad_in.reshape(512, 512), grad_out.reshape(512, 512), grad_gain[:4].reshape(512))


def solution(mesh):
    return jax.shard_map(
        shards,
        mesh=mesh,
        in_specs=(P("rows", None), P("rows", "rep"), P(), P(), P(), P("rows", None)),
        out_specs=(P("rows", None), P("rows", None), P(), P(), P()),
        check_vma=False,
    )
```

```python
import jax
import jax.numpy as jnp
from jax import lax
from jax.experimental import pallas as pl
from jax.experimental.pallas import tpu as pltpu
from jax.sharding import PartitionSpec as P


BF = jnp.bfloat16
F32 = jnp.float32
ALL = ("rows", "rep")


def place(u, v, p):
    z, y = (v, u) if p % 2 == 0 else (u, v)
    return (8 * z + y) * 8 + p


E8 = range(8)
ALONG_U = [[place(u, v, p) for u in E8] for v in E8 for p in E8]
ALONG_V = [[place(u, v, p) for v in E8] for u in E8 for p in E8]
OUT = [((8 * z + y) * 8 + t, place(t, y, z)) for z in E8 for y in E8 for t in E8]
BACK = [(b, a) for a, b in OUT]
CORE = [(i, i ^ 1) for i in range(512)]
SHIFT_X = [[(i, (i & ~7) | ((i + 2 * d) & 7)) for i in range(512)] for d in (1, 2, 3)]


def dot(a, b, ca, cb):
    return lax.dot_general(a, b, (((ca,), (cb,)), ((), ())), preferred_element_type=F32)


def trade(x, groups):
    return lax.all_to_all(x, ALL, 0, 0, axis_index_groups=groups)


def call(body, outs, *args, scratch=()):
    return pl.pallas_call(
        body,
        out_shape=[jax.ShapeDtypeStruct(s, d) for s, d in outs],
        in_specs=[pl.BlockSpec(memory_space=pltpu.VMEM)] * len(args),
        out_specs=[pl.BlockSpec(memory_space=pltpu.VMEM)] * len(outs),
        scratch_shapes=list(scratch),
        compiler_params=pltpu.CompilerParams(vmem_limit_bytes=40 * 1024 * 1024),
    )(*args)


def is_core_0():
    return (lax.axis_index("rep") & 1) == 0


def left_half():
    return lax.broadcasted_iota(jnp.int32, (1, 128), 1) < 64


def total_of(got):
    total = got[0].astype(F32)
    for i in range(1, 8):
        total = total + got[i].astype(F32)
    return total


def sum_and_copy(got, cot, send):
    total, piece = total_of(got).astype(BF), cot[...]
    for u in E8:
        send[u, 0:128, :] = total
        send[u, 128:144, :] = piece


def update(got, gain_ref, w_in_ref, w_out_ref, out_ref, send, change, rows, columns):
    summed = got[0, 0:128, :].astype(F32)
    for i in range(1, 8):
        summed = summed + got[i, 0:128, :].astype(F32)
    r = lax.axis_index("rows")
    first = is_core_0()
    u = jnp.where(first, r & 7, r >> 3)
    gain = gain_ref[...]
    w_in, w_out = w_in_ref[...], w_out_ref[...]
    cot = got[:, 128:144, :].reshape(128, 512)
    scale = lax.rsqrt(jnp.mean(summed * summed, axis=-1, keepdims=True) + 1e-05)
    normed = summed * scale
    lifted = (normed * gain).astype(BF)
    pre = dot(lifted, w_in, 1, 0)
    grad_hidden = dot(cot, w_out, 1, 1)
    sigma = jax.nn.sigmoid(pre)
    hidden = (pre * sigma).astype(BF)
    grad_pre = (grad_hidden * sigma * (1.0 + pre * (1.0 - sigma))).astype(BF)
    grad_lifted = dot(grad_pre, w_in, 1, 1)
    change[...] = dot(hidden, w_out, 1, 0).astype(BF)
    out_ref[...] = change[pl.ds(pl.multiple_of(u * 16, 16), 16), :]
    gain_row = jnp.sum(grad_lifted * normed, axis=0, keepdims=True)
    gain_high = gain_row.astype(BF).astype(F32)
    gain_rows = jnp.concatenate([jnp.zeros((14, 512), F32), gain_high, gain_row - gain_high], axis=0)
    grad_normed = grad_lifted * gain
    grad_summed = (
        scale * (grad_normed - normed * jnp.mean(grad_normed * normed, axis=-1, keepdims=True))
    ).astype(BF)
    for v in E8:
        send[v, 0:128, :] = grad_summed
    left = left_half()
    top = lax.broadcasted_iota(jnp.int32, (16, 1), 0) < 14

    def pairs(a, b, ref):
        a, b = a.astype(F32), b.astype(F32)
        for m in range(4):
            one, two = a[:, 128 * m : 128 * m + 128], b[:, 128 * m : 128 * m + 128]
            ref[2 * m] = jnp.where(left, one, pltpu.roll(two, 64, 1)).astype(BF)
            ref[2 * m + 1] = jnp.where(left, pltpu.roll(one, 64, 1), two).astype(BF)

    pairs(lifted, hidden, rows)
    pairs(grad_pre, cot, columns)
    for k in E8:
        tile = dot(rows[jnp.where(first, k, u)], columns[jnp.where(first, u, k)], 0, 0)
        tile = jnp.where(left, tile[0:64], tile[64:128])
        high = tile.astype(BF)
        low = tile - high.astype(F32)
        for j in range(4):
            at = slice(128 * j, 128 * j + 128)
            send[k, 128:144, at] = high[16 * j : 16 * j + 16]
            send[k, 144:160, at] = jnp.where(top, low[16 * j : 16 * j + 16], gain_rows[:, at]).astype(BF)


def back_and_tile(adjacency, got, nodes, change, send, out):
    own = nodes[pl.ds(pl.multiple_of(lax.axis_index("rep") * 16, 16), 16), :].astype(F32)
    final = (own + change[...].astype(F32)).astype(BF)
    for j in range(4):
        out[16 * j : 16 * j + 16, :] = final[:, 128 * j : 128 * j + 128]
    field = got[:, 0:128, :].reshape(1024, 512)
    back = dot(adjacency[...], field, 1, 0)
    for q in E8:
        for j in range(4):
            send[q, 16 * j : 16 * j + 16, :] = back[16 * q : 16 * q + 16, 128 * j : 128 * j + 128].astype(BF)
    exact, lows = jnp.zeros((16, 512), F32), jnp.zeros((16, 512), F32)
    for v in E8:
        exact = exact + got[v, 128:144, :].astype(F32)
        lows = lows + got[v, 144:160, :].astype(F32)
    exact = exact + jnp.where(lax.broadcasted_iota(jnp.int32, (16, 1), 0) < 14, lows, 0.0)
    gain = lows[14:15] + lows[15:16]
    gain = jnp.concatenate([gain[:, 128 * j : 128 * j + 128] for j in range(4)] + [jnp.zeros((4, 128), F32)], axis=0)
    high = exact.astype(BF)
    low = (exact - high.astype(F32)).astype(BF)
    gain_high = gain.astype(BF).astype(F32)
    gain = jnp.concatenate([gain_high, gain - gain_high], axis=0).astype(BF)
    for q in E8:
        for i in range(2):
            j = 2 * (q % 2) + i
            send[q, 64 + 16 * i : 80 + 16 * i, :] = high[:, 128 * j : 128 * j + 128]
            send[q, 96 + 16 * i : 112 + 16 * i, :] = low[:, 128 * j : 128 * j + 128]
        send[q, 128:144, :] = gain


def add_up(got, cotangent, out, piece, send, gain):
    total = total_of(got)
    own = cotangent[pl.ds(pl.multiple_of(lax.axis_index("rep") * 16, 16), 16), :].astype(F32)
    for j in range(4):
        piece[16 * j : 16 * j + 16, :] = (
            own[:, 128 * j : 128 * j + 128] + total[16 * j : 16 * j + 16]
        ).astype(BF)
    piece[64:128, :] = out[...]
    block = (total[64:96] + total[96:128]).astype(BF)
    for r in range(64):
        send[r] = block
    gain[...] = total[128:136] + total[136:144]


def lay_rows(src, z, grad_in, grad_out):
    left = left_half()
    for m in range(4):
        even, odd = src[8 * z + 2 * m].astype(F32), src[8 * z + 2 * m + 1].astype(F32)
        cols = slice(128 * m, 128 * m + 128)
        grad_in[z, :, cols] = jnp.where(left, even, pltpu.roll(odd, 64, 1))
        grad_out[z, :, cols] = jnp.where(left, pltpu.roll(even, 64, 1), odd)


def lay(src, p0, p1, p2, p3, grad_in, grad_out, node_grad, node_out):
    for z in E8:
        lay_rows(src, z, grad_in, grad_out)
    p = lax.axis_index("rep")
    c = p & 1
    for d, pieces in enumerate((p0, p1, p2, p3)):
        for h in range(2):
            q = (((p >> 1) + 4 - d) & 3) * 2 + (c ^ h)
            rows = pl.ds(pl.multiple_of(16 * q, 16), 16)
            for j in range(4):
                cols = slice(128 * j, 128 * j + 128)
                node_grad[rows, cols] = pieces[h, 16 * j : 16 * j + 16, :]
                node_out[rows, cols] = pieces[h, 64 + 16 * j : 80 + 16 * j, :]


def lay_both(src, mine_in, mine_out, grad_in, grad_out, part_in, part_out, sems):
    c = lax.axis_index("rep") & 1
    copies = []

    def send(a, b, z, at):
        copies.append(pltpu.make_async_copy(a.at[z], b.at[z, at], sems.at[len(copies)]))
        copies[-1].start()

    for z in E8:
        send(mine_in, grad_in, z, c)
        send(mine_out, grad_out, z, c)
    for z in E8:
        lay_rows(src, z, part_in, part_out)
        send(part_in, grad_in, z, 1 - c)
        send(part_out, grad_out, z, 1 - c)
    for copy in copies:
        copy.wait()


def shards(nodes, adjacency, gain, w_in, w_out, cotangent):
    piece = lax.dynamic_slice_in_dim(cotangent, lax.axis_index("rep") * 16, 16, 0)
    cot = lax.ppermute(piece, ALL, OUT)

    part = dot(adjacency, nodes, 0, 0).astype(BF).reshape(8, 128, 512)
    (part,) = call(sum_and_copy, [((8, 144, 512), BF)], trade(part, ALONG_V), cot)
    got = trade(part, ALONG_U)

    change, send = call(
        update,
        [((16, 512), BF), ((8, 160, 512), BF)],
        got, gain.reshape(1, 512), w_in, w_out,
        scratch=[pltpu.VMEM((128, 512), BF)] + [pltpu.VMEM((8, 128, 128), BF)] * 2,
    )
    change = lax.ppermute(change, ALL, BACK)
    send, out = call(
        back_and_tile, [((8, 144, 128), BF), ((64, 128), BF)],
        adjacency, trade(send, ALONG_V), nodes, change,
    )
    piece, send, grad_gain = call(
        add_up, [((128, 128), BF), ((64, 32, 128), BF), ((8, 128), F32)],
        lax.all_to_all(send, "rep", 0, 0), cotangent, out,
    )
    mine = lax.all_to_all(send, "rows", 0, 0)
    pieces = jnp.stack([piece, lax.ppermute(piece, ALL, CORE)])
    pieces = [pieces] + [lax.ppermute(pieces, ALL, perm) for perm in SHIFT_X]
    mine, pieces = lax.optimization_barrier((mine, pieces))
    other = lax.ppermute(mine, ALL, CORE)
    half = ((8, 32, 512), F32)
    mine_in, mine_out, node_grad, node_out = call(
        lay, [half, half, ((128, 512), BF), ((128, 512), BF)], mine, *pieces
    )
    whole = jax.ShapeDtypeStruct((8, 2, 32, 512), F32)
    vmem = pl.BlockSpec(memory_space=pltpu.VMEM)
    grad_in, grad_out = pl.pallas_call(
        lay_both,
        out_shape=[whole, whole],
        in_specs=[vmem] * 3,
        out_specs=[pl.BlockSpec(memory_space=pl.ANY)] * 2,
        scratch_shapes=[pltpu.VMEM(*half)] * 2 + [pltpu.SemaphoreType.DMA((32,))],
        compiler_params=pltpu.CompilerParams(vmem_limit_bytes=40 * 1024 * 1024),
    )(other, mine_in, mine_out)
    return (node_out, node_grad, grad_in.reshape(512, 512), grad_out.reshape(512, 512), grad_gain[:4].reshape(512))


def solution(mesh):
    return jax.shard_map(
        shards,
        mesh=mesh,
        in_specs=(P("rows", None), P("rows", "rep"), P(), P(), P(), P("rows", None)),
        out_specs=(P("rows", None), P("rows", None), P(), P(), P()),
        check_vma=False,
    )
```

```python
import jax
import jax.numpy as jnp
from jax import lax
from jax.experimental import pallas as pl
from jax.experimental.pallas import tpu as pltpu
from jax.sharding import PartitionSpec as P


BF = jnp.bfloat16
F32 = jnp.float32
ALL = ("rows", "rep")


E8 = range(8)
ORDER = (0, 2, 4, 6, 1, 3, 5, 7)


def label(i):
    return (i >> 1) | ((i & 1) << 2)


def place(u, v, p):
    z, y = (ORDER[v], ORDER[u]) if p % 2 == 0 else (ORDER[u], ORDER[v])
    return (8 * z + y) * 8 + p


assert all(label(ORDER[i]) == i for i in E8)
ALONG_U = [[place(u, v, p) for u in E8] for v in E8 for p in E8]
PLANES = [[(8 * z + y) * 8 + p for z in ORDER for y in ORDER] for p in E8]
ALONG_V = [[place(u, v, p) for v in E8] for u in E8 for p in E8]
OUT = [((8 * z + y) * 8 + t, place(t, y, z)) for z in E8 for y in E8 for t in E8]
BACK = [(b, a) for a, b in OUT]
CORE = [(i, i ^ 1) for i in range(512)]
SHIFT_X = [[(i, (i & ~7) | ((i + 2 * d) & 7)) for i in range(512)] for d in (1, 2, 3)]


def dot(a, b, ca, cb):
    return lax.dot_general(a, b, (((ca,), (cb,)), ((), ())), preferred_element_type=F32)


def trade(x, groups):
    return lax.all_to_all(x, ALL, 0, 0, axis_index_groups=groups)


def call(body, outs, *args, scratch=()):
    return pl.pallas_call(
        body,
        out_shape=[jax.ShapeDtypeStruct(s, d) for s, d in outs],
        in_specs=[pl.BlockSpec(memory_space=pltpu.VMEM)] * len(args),
        out_specs=[pl.BlockSpec(memory_space=pltpu.VMEM)] * len(outs),
        scratch_shapes=list(scratch),
        compiler_params=pltpu.CompilerParams(vmem_limit_bytes=40 * 1024 * 1024),
    )(*args)


def is_core_0():
    return (lax.axis_index("rep") & 1) == 0


def left_half():
    return lax.broadcasted_iota(jnp.int32, (1, 128), 1) < 64


def total_of(got):
    total = got[0].astype(F32)
    for i in range(1, 8):
        total = total + got[i].astype(F32)
    return total


def sum_and_copy(got, cot, send):
    total, piece = total_of(got).astype(BF), cot[...]
    for u in E8:
        send[u, 0:128, :] = total
        send[u, 128:144, :] = piece


def update(got, gain_ref, w_in_ref, w_out_ref, out_ref, send, change, rows, columns):
    summed = got[0, 0:128, :].astype(F32)
    for i in range(1, 8):
        summed = summed + got[i, 0:128, :].astype(F32)
    r = lax.axis_index("rows")
    first = is_core_0()
    u = label(jnp.where(first, r & 7, r >> 3))
    gain = gain_ref[...]
    w_in, w_out = w_in_ref[...], w_out_ref[...]
    cot = got[:, 128:144, :].reshape(128, 512)
    scale = lax.rsqrt(jnp.mean(summed * summed, axis=-1, keepdims=True) + 1e-05)
    normed = summed * scale
    lifted = (normed * gain).astype(BF)
    pre = dot(lifted, w_in, 1, 0)
    grad_hidden = dot(cot, w_out, 1, 1)
    sigma = jax.nn.sigmoid(pre)
    hidden = (pre * sigma).astype(BF)
    grad_pre = (grad_hidden * sigma * (1.0 + pre * (1.0 - sigma))).astype(BF)
    grad_lifted = dot(grad_pre, w_in, 1, 1)
    change[...] = dot(hidden, w_out, 1, 0).astype(BF)
    out_ref[...] = change[pl.ds(pl.multiple_of(u * 16, 16), 16), :]
    gain_row = jnp.sum(grad_lifted * normed, axis=0, keepdims=True)
    gain_high = gain_row.astype(BF).astype(F32)
    gain_rows = jnp.concatenate([jnp.zeros((14, 512), F32), gain_high, gain_row - gain_high], axis=0)
    grad_normed = grad_lifted * gain
    grad_summed = (
        scale * (grad_normed - normed * jnp.mean(grad_normed * normed, axis=-1, keepdims=True))
    ).astype(BF)
    for v in E8:
        send[v, 0:128, :] = grad_summed
    left = left_half()
    top = lax.broadcasted_iota(jnp.int32, (16, 1), 0) < 14

    def pairs(a, b, ref):
        a, b = a.astype(F32), b.astype(F32)
        for m in range(4):
            one, two = a[:, 128 * m : 128 * m + 128], b[:, 128 * m : 128 * m + 128]
            ref[2 * m] = jnp.where(left, one, pltpu.roll(two, 64, 1)).astype(BF)
            ref[2 * m + 1] = jnp.where(left, pltpu.roll(one, 64, 1), two).astype(BF)

    pairs(lifted, hidden, rows)
    pairs(grad_pre, cot, columns)
    for k in E8:
        tile = dot(rows[jnp.where(first, k, u)], columns[jnp.where(first, u, k)], 0, 0)
        tile = jnp.where(left, tile[0:64], tile[64:128])
        high = tile.astype(BF)
        low = tile - high.astype(F32)
        for j in range(4):
            at = slice(128 * j, 128 * j + 128)
            send[k, 128:144, at] = high[16 * j : 16 * j + 16]
            send[k, 144:160, at] = jnp.where(top, low[16 * j : 16 * j + 16], gain_rows[:, at]).astype(BF)


def back_and_tile(adjacency, got, nodes, change, send, out):
    own = nodes[pl.ds(pl.multiple_of(lax.axis_index("rep") * 16, 16), 16), :].astype(F32)
    final = (own + change[...].astype(F32)).astype(BF)
    for j in range(4):
        out[16 * j : 16 * j + 16, :] = final[:, 128 * j : 128 * j + 128]
    field = got[:, 0:128, :].reshape(1024, 512)
    back = dot(adjacency[...], field, 1, 0)
    for q in E8:
        for j in range(4):
            send[q, 16 * j : 16 * j + 16, :] = back[16 * q : 16 * q + 16, 128 * j : 128 * j + 128].astype(BF)
    exact, lows = jnp.zeros((16, 512), F32), jnp.zeros((16, 512), F32)
    for v in E8:
        exact = exact + got[v, 128:144, :].astype(F32)
        lows = lows + got[v, 144:160, :].astype(F32)
    exact = exact + jnp.where(lax.broadcasted_iota(jnp.int32, (16, 1), 0) < 14, lows, 0.0)
    gain = lows[14:15] + lows[15:16]
    gain = jnp.concatenate([gain[:, 128 * j : 128 * j + 128] for j in range(4)] + [jnp.zeros((4, 128), F32)], axis=0)
    high = exact.astype(BF)
    low = (exact - high.astype(F32)).astype(BF)
    gain_high = gain.astype(BF).astype(F32)
    gain = jnp.concatenate([gain_high, gain - gain_high], axis=0).astype(BF)
    for q in E8:
        for i in range(2):
            j = 2 * (q % 2) + i
            send[q, 64 + 16 * i : 80 + 16 * i, :] = high[:, 128 * j : 128 * j + 128]
            send[q, 96 + 16 * i : 112 + 16 * i, :] = low[:, 128 * j : 128 * j + 128]
        send[q, 128:144, :] = gain


def add_up(got, cotangent, out, piece, send, gain):
    total = total_of(got)
    own = cotangent[pl.ds(pl.multiple_of(lax.axis_index("rep") * 16, 16), 16), :].astype(F32)
    for j in range(4):
        piece[16 * j : 16 * j + 16, :] = (
            own[:, 128 * j : 128 * j + 128] + total[16 * j : 16 * j + 16]
        ).astype(BF)
    piece[64:128, :] = out[...]
    block = (total[64:96] + total[96:128]).astype(BF)
    for r in range(64):
        send[r] = block
    gain[...] = total[128:136] + total[136:144]


def lay_rows(src, z, grad_in, grad_out):
    left = left_half()
    for m in range(4):
        even, odd = src[8 * z + 2 * m].astype(F32), src[8 * z + 2 * m + 1].astype(F32)
        cols = slice(128 * m, 128 * m + 128)
        grad_in[z, :, cols] = jnp.where(left, even, pltpu.roll(odd, 64, 1))
        grad_out[z, :, cols] = jnp.where(left, pltpu.roll(even, 64, 1), odd)


def lay(src, p0, p1, p2, p3, grad_in, grad_out, node_grad, node_out):
    for z in E8:
        lay_rows(src, z, grad_in, grad_out)
    p = lax.axis_index("rep")
    c = p & 1
    for d, pieces in enumerate((p0, p1, p2, p3)):
        for h in range(2):
            q = (((p >> 1) + 4 - d) & 3) * 2 + (c ^ h)
            rows = pl.ds(pl.multiple_of(16 * q, 16), 16)
            for j in range(4):
                cols = slice(128 * j, 128 * j + 128)
                node_grad[rows, cols] = pieces[h, 16 * j : 16 * j + 16, :]
                node_out[rows, cols] = pieces[h, 64 + 16 * j : 80 + 16 * j, :]


def lay_both(src, mine_in, mine_out, grad_in, grad_out, part_in, part_out, sems):
    c = lax.axis_index("rep") & 1
    copies = []

    def send(a, b, z, at):
        copies.append(pltpu.make_async_copy(a.at[z], b.at[z, at], sems.at[len(copies)]))
        copies[-1].start()

    for z in E8:
        send(mine_in, grad_in, z, c)
        send(mine_out, grad_out, z, c)
    for z in E8:
        lay_rows(src, z, part_in, part_out)
        send(part_in, grad_in, z, 1 - c)
        send(part_out, grad_out, z, 1 - c)
    for copy in copies:
        copy.wait()


def shards(nodes, adjacency, gain, w_in, w_out, cotangent):
    piece = lax.dynamic_slice_in_dim(cotangent, lax.axis_index("rep") * 16, 16, 0)
    cot = lax.ppermute(piece, ALL, OUT)

    part = dot(adjacency, nodes, 0, 0).astype(BF).reshape(8, 128, 512)
    (part,) = call(sum_and_copy, [((8, 144, 512), BF)], trade(part, ALONG_V), cot)
    got = trade(part, ALONG_U)

    change, send = call(
        update,
        [((16, 512), BF), ((8, 160, 512), BF)],
        got, gain.reshape(1, 512), w_in, w_out,
        scratch=[pltpu.VMEM((128, 512), BF)] + [pltpu.VMEM((8, 128, 128), BF)] * 2,
    )
    change = lax.ppermute(change, ALL, BACK)
    send, out = call(
        back_and_tile, [((8, 144, 128), BF), ((64, 128), BF)],
        adjacency, trade(send, ALONG_V), nodes, change,
    )
    piece, send, grad_gain = call(
        add_up, [((128, 128), BF), ((64, 32, 128), BF), ((8, 128), F32)],
        lax.all_to_all(send, "rep", 0, 0), cotangent, out,
    )
    mine = trade(send, PLANES)
    pieces = jnp.stack([piece, lax.ppermute(piece, ALL, CORE)])
    pieces = [pieces] + [lax.ppermute(pieces, ALL, perm) for perm in SHIFT_X]
    mine, pieces = lax.optimization_barrier((mine, pieces))
    other = lax.ppermute(mine, ALL, CORE)
    half = ((8, 32, 512), F32)
    mine_in, mine_out, node_grad, node_out = call(
        lay, [half, half, ((128, 512), BF), ((128, 512), BF)], mine, *pieces
    )
    whole = jax.ShapeDtypeStruct((8, 2, 32, 512), F32)
    vmem = pl.BlockSpec(memory_space=pltpu.VMEM)
    grad_in, grad_out = pl.pallas_call(
        lay_both,
        out_shape=[whole, whole],
        in_specs=[vmem] * 3,
        out_specs=[pl.BlockSpec(memory_space=pl.ANY)] * 2,
        scratch_shapes=[pltpu.VMEM(*half)] * 2 + [pltpu.SemaphoreType.DMA((32,))],
        compiler_params=pltpu.CompilerParams(vmem_limit_bytes=40 * 1024 * 1024),
    )(other, mine_in, mine_out)
    return (node_out, node_grad, grad_in.reshape(512, 512), grad_out.reshape(512, 512), grad_gain[:4].reshape(512))


def solution(mesh):
    return jax.shard_map(
        shards,
        mesh=mesh,
        in_specs=(P("rows", None), P("rows", "rep"), P(), P(), P(), P("rows", None)),
        out_specs=(P("rows", None), P("rows", None), P(), P(), P()),
        check_vma=False,
    )
```

```python
import jax
import jax.numpy as jnp
from jax import lax
from jax.experimental import pallas as pl
from jax.experimental.pallas import tpu as pltpu
from jax.sharding import PartitionSpec as P


BF = jnp.bfloat16
F32 = jnp.float32
ALL = ("rows", "rep")


E8 = range(8)
ORDER = (0, 2, 4, 6, 1, 3, 5, 7)


def label(i):
    return (i >> 1) | ((i & 1) << 2)


def place(u, v, p):
    z, y = (ORDER[v], ORDER[u]) if p % 2 == 0 else (ORDER[u], ORDER[v])
    return (8 * z + y) * 8 + p


assert all(label(ORDER[i]) == i for i in E8)
ALONG_U = [[place(u, v, p) for u in E8] for v in E8 for p in E8]
PLANES = [[(8 * z + y) * 8 + p for z in ORDER for y in ORDER] for p in E8]
ALONG_V = [[place(u, v, p) for v in E8] for u in E8 for p in E8]
OUT = [((8 * z + y) * 8 + t, place(t, y, z)) for z in E8 for y in E8 for t in E8]
BACK = [(b, a) for a, b in OUT]
CORE = [(i, i ^ 1) for i in range(512)]
SHIFT_X = [[(i, (i & ~7) | ((i + 2 * d) & 7)) for i in range(512)] for d in (1, 2, 3)]


def dot(a, b, ca, cb):
    return lax.dot_general(a, b, (((ca,), (cb,)), ((), ())), preferred_element_type=F32)


def trade(x, groups):
    return lax.all_to_all(x, ALL, 0, 0, axis_index_groups=groups)


def call(body, outs, *args, scratch=()):
    return pl.pallas_call(
        body,
        out_shape=[jax.ShapeDtypeStruct(s, d) for s, d in outs],
        in_specs=[pl.BlockSpec(memory_space=pltpu.VMEM)] * len(args),
        out_specs=[pl.BlockSpec(memory_space=pltpu.VMEM)] * len(outs),
        scratch_shapes=list(scratch),
        compiler_params=pltpu.CompilerParams(vmem_limit_bytes=40 * 1024 * 1024),
    )(*args)


def is_core_0():
    return (lax.axis_index("rep") & 1) == 0


def left_half():
    return lax.broadcasted_iota(jnp.int32, (1, 128), 1) < 64


def total_of(got):
    total = got[0].astype(F32)
    for i in range(1, 8):
        total = total + got[i].astype(F32)
    return total


def sum_and_copy(got, cot, send):
    total, piece = total_of(got).astype(BF), cot[...]
    for u in E8:
        send[u, 0:128, :] = total
        send[u, 128:144, :] = piece


def update(got, gain_ref, w_in_ref, w_out_ref, out_ref, send, change, rows, columns):
    summed = got[0, 0:128, :].astype(F32)
    for i in range(1, 8):
        summed = summed + got[i, 0:128, :].astype(F32)
    r = lax.axis_index("rows")
    first = is_core_0()
    u = label(jnp.where(first, r & 7, r >> 3))
    gain = gain_ref[...]
    w_in, w_out = w_in_ref[...], w_out_ref[...]
    cot = got[:, 128:144, :].reshape(128, 512)
    scale = lax.rsqrt(jnp.mean(summed * summed, axis=-1, keepdims=True) + 1e-05)
    normed = summed * scale
    lifted = (normed * gain).astype(BF)
    pre = dot(lifted, w_in, 1, 0)
    grad_hidden = dot(cot, w_out, 1, 1)
    sigma = jax.nn.sigmoid(pre)
    hidden = (pre * sigma).astype(BF)
    grad_pre = (grad_hidden * sigma * (1.0 + pre * (1.0 - sigma))).astype(BF)
    grad_lifted = dot(grad_pre, w_in, 1, 1)
    change[...] = dot(hidden, w_out, 1, 0).astype(BF)
    out_ref[...] = change[pl.ds(pl.multiple_of(u * 16, 16), 16), :]
    gain_row = jnp.sum(grad_lifted * normed, axis=0, keepdims=True)
    gain_high = gain_row.astype(BF).astype(F32)
    gain_rows = jnp.concatenate([jnp.zeros((14, 512), F32), gain_high, gain_row - gain_high], axis=0)
    grad_normed = grad_lifted * gain
    grad_summed = (
        scale * (grad_normed - normed * jnp.mean(grad_normed * normed, axis=-1, keepdims=True))
    ).astype(BF)
    for v in E8:
        send[v, 0:128, :] = grad_summed
    left = left_half()
    top = lax.broadcasted_iota(jnp.int32, (16, 1), 0) < 14

    def pairs(a, b, ref):
        a, b = a.astype(F32), b.astype(F32)
        for m in range(4):
            one, two = a[:, 128 * m : 128 * m + 128], b[:, 128 * m : 128 * m + 128]
            ref[2 * m] = jnp.where(left, one, pltpu.roll(two, 64, 1)).astype(BF)
            ref[2 * m + 1] = jnp.where(left, pltpu.roll(one, 64, 1), two).astype(BF)

    pairs(lifted, hidden, rows)
    pairs(grad_pre, cot, columns)
    for k in E8:
        tile = dot(rows[jnp.where(first, k, u)], columns[jnp.where(first, u, k)], 0, 0)
        tile = jnp.where(left, tile[0:64], tile[64:128])
        high = tile.astype(BF)
        low = tile - high.astype(F32)
        for j in range(4):
            at = slice(128 * j, 128 * j + 128)
            send[k, 128:144, at] = high[16 * j : 16 * j + 16]
            send[k, 144:160, at] = jnp.where(top, low[16 * j : 16 * j + 16], gain_rows[:, at]).astype(BF)


def back_and_tile(adjacency, got, nodes, change, send, out):
    own = nodes[pl.ds(pl.multiple_of(lax.axis_index("rep") * 16, 16), 16), :].astype(F32)
    final = (own + change[...].astype(F32)).astype(BF)
    for j in range(4):
        out[16 * j : 16 * j + 16, :] = final[:, 128 * j : 128 * j + 128]
    field = got[:, 0:128, :].reshape(1024, 512)
    back = dot(adjacency[...], field, 1, 0)
    for q in E8:
        for j in range(4):
            send[q, 16 * j : 16 * j + 16, :] = back[16 * q : 16 * q + 16, 128 * j : 128 * j + 128].astype(BF)
    exact, lows = jnp.zeros((16, 512), F32), jnp.zeros((16, 512), F32)
    for v in E8:
        exact = exact + got[v, 128:144, :].astype(F32)
        lows = lows + got[v, 144:160, :].astype(F32)
    exact = exact + jnp.where(lax.broadcasted_iota(jnp.int32, (16, 1), 0) < 14, lows, 0.0)
    gain = lows[14:15] + lows[15:16]
    gain = jnp.concatenate([gain[:, 128 * j : 128 * j + 128] for j in range(4)], axis=0)
    gain_high = gain.astype(BF).astype(F32)
    gain = jnp.concatenate([jnp.zeros((8, 128), F32), gain_high, gain - gain_high], axis=0)
    high = exact.astype(BF)
    low = exact - high.astype(F32)
    top = lax.broadcasted_iota(jnp.int32, (16, 1), 0) < 8
    for q in E8:
        for i in range(2):
            at = slice(128 * (2 * (q % 2) + i), 128 * (2 * (q % 2) + i) + 128)
            send[q, 64 + 16 * i : 80 + 16 * i, :] = high[:, at]
            send[q, 96 + 16 * i : 112 + 16 * i, :] = (low[:, at] if i == 0 else jnp.where(top, low[:, at], gain)).astype(BF)


def add_up(got, cotangent, out, piece, send, gain):
    total = total_of(got)
    own = cotangent[pl.ds(pl.multiple_of(lax.axis_index("rep") * 16, 16), 16), :].astype(F32)
    for j in range(4):
        piece[16 * j : 16 * j + 16, :] = (
            own[:, 128 * j : 128 * j + 128] + total[16 * j : 16 * j + 16]
        ).astype(BF)
    piece[64:128, :] = out[...]
    block = jnp.concatenate([total[64:88] + total[96:120], total[88:96]], axis=0).astype(BF)
    for r in range(64):
        send[r] = block
    for j in range(4):
        gain[0:1, 128 * j : 128 * j + 128] = total[120 + j : 121 + j] + total[124 + j : 125 + j]


def lay_rows(src, z, grad_in, grad_out):
    left = left_half()
    for m in range(4):
        even, odd = src[8 * z + 2 * m].astype(F32), src[8 * z + 2 * m + 1].astype(F32)
        cols = slice(128 * m, 128 * m + 128)
        grad_in[z, :, cols] = jnp.where(left, even, pltpu.roll(odd, 64, 1))
        grad_out[z, :, cols] = jnp.where(left, pltpu.roll(even, 64, 1), odd)


def lay(src, p0, p1, p2, p3, grad_in, grad_out, node_grad, node_out):
    for z in E8:
        lay_rows(src, z, grad_in, grad_out)
    p = lax.axis_index("rep")
    c = p & 1
    for d, pieces in enumerate((p0, p1, p2, p3)):
        for h in range(2):
            q = (((p >> 1) + 4 - d) & 3) * 2 + (c ^ h)
            rows = pl.ds(pl.multiple_of(16 * q, 16), 16)
            for j in range(4):
                cols = slice(128 * j, 128 * j + 128)
                node_grad[rows, cols] = pieces[h, 16 * j : 16 * j + 16, :]
                node_out[rows, cols] = pieces[h, 64 + 16 * j : 80 + 16 * j, :]


def lay_both(src, mine_in, mine_out, grad_in, grad_out, part_in, part_out, sems):
    c = lax.axis_index("rep") & 1
    copies = []

    def send(a, b, z, at):
        copies.append(pltpu.make_async_copy(a.at[z], b.at[z, at], sems.at[len(copies)]))
        copies[-1].start()

    for z in E8:
        send(mine_in, grad_in, z, c)
        send(mine_out, grad_out, z, c)
    for z in E8:
        lay_rows(src, z, part_in, part_out)
        send(part_in, grad_in, z, 1 - c)
        send(part_out, grad_out, z, 1 - c)
    for copy in copies:
        copy.wait()


def shards(nodes, adjacency, gain, w_in, w_out, cotangent):
    piece = lax.dynamic_slice_in_dim(cotangent, lax.axis_index("rep") * 16, 16, 0)
    cot = lax.ppermute(piece, ALL, OUT)

    part = dot(adjacency, nodes, 0, 0).astype(BF).reshape(8, 128, 512)
    (part,) = call(sum_and_copy, [((8, 144, 512), BF)], trade(part, ALONG_V), cot)
    got = trade(part, ALONG_U)

    change, send = call(
        update,
        [((16, 512), BF), ((8, 160, 512), BF)],
        got, gain.reshape(1, 512), w_in, w_out,
        scratch=[pltpu.VMEM((128, 512), BF)] + [pltpu.VMEM((8, 128, 128), BF)] * 2,
    )
    change = lax.ppermute(change, ALL, BACK)
    send, out = call(
        back_and_tile, [((8, 128, 128), BF), ((64, 128), BF)],
        adjacency, trade(send, ALONG_V), nodes, change,
    )
    piece, send, grad_gain = call(
        add_up, [((128, 128), BF), ((64, 32, 128), BF), ((1, 512), F32)],
        lax.all_to_all(send, "rep", 0, 0), cotangent, out,
    )
    mine = trade(send, PLANES)
    pieces = jnp.stack([piece, lax.ppermute(piece, ALL, CORE)])
    pieces = [pieces] + [lax.ppermute(pieces, ALL, perm) for perm in SHIFT_X]
    mine, pieces = lax.optimization_barrier((mine, pieces))
    other = lax.ppermute(mine, ALL, CORE)
    half = ((8, 32, 512), F32)
    mine_in, mine_out, node_grad, node_out = call(
        lay, [half, half, ((128, 512), BF), ((128, 512), BF)], mine, *pieces
    )
    whole = jax.ShapeDtypeStruct((8, 2, 32, 512), F32)
    vmem = pl.BlockSpec(memory_space=pltpu.VMEM)
    grad_in, grad_out = pl.pallas_call(
        lay_both,
        out_shape=[whole, whole],
        in_specs=[vmem] * 3,
        out_specs=[pl.BlockSpec(memory_space=pl.ANY)] * 2,
        scratch_shapes=[pltpu.VMEM(*half)] * 2 + [pltpu.SemaphoreType.DMA((32,))],
        compiler_params=pltpu.CompilerParams(vmem_limit_bytes=40 * 1024 * 1024),
    )(other, mine_in, mine_out)
    return (node_out, node_grad, grad_in.reshape(512, 512), grad_out.reshape(512, 512), grad_gain.reshape(512))


def solution(mesh):
    return jax.shard_map(
        shards,
        mesh=mesh,
        in_specs=(P("rows", None), P("rows", "rep"), P(), P(), P(), P("rows", None)),
        out_specs=(P("rows", None), P("rows", None), P(), P(), P()),
        check_vma=False,
    )
```

```python
import jax
import jax.numpy as jnp
from jax import lax
from jax.experimental import pallas as pl
from jax.experimental.pallas import tpu as pltpu
from jax.sharding import PartitionSpec as P


BF = jnp.bfloat16
F32 = jnp.float32
ALL = ("rows", "rep")


E8 = range(8)
ORDER = (0, 2, 4, 6, 1, 3, 5, 7)


def label(i):
    return (i >> 1) | ((i & 1) << 2)


def place(u, v, p):
    z, y = (ORDER[v], ORDER[u]) if p % 2 == 0 else (ORDER[u], ORDER[v])
    return (8 * z + y) * 8 + p


assert all(label(ORDER[i]) == i for i in E8)
ALONG_U = [[place(u, v, p) for u in E8] for v in E8 for p in E8]
PLANES = [[(8 * z + y) * 8 + p for z in ORDER for y in ORDER] for p in E8]
ALONG_V = [[place(u, v, p) for v in E8] for u in E8 for p in E8]
OUT = [((8 * z + y) * 8 + t, place(t, y, z)) for z in E8 for y in E8 for t in E8]
BACK = [(b, a) for a, b in OUT]
CORE = [(i, i ^ 1) for i in range(512)]
SHIFT_X = [[(i, (i & ~7) | ((i + 2 * d) & 7)) for i in range(512)] for d in (1, 2, 3)]


def dot(a, b, ca, cb):
    return lax.dot_general(a, b, (((ca,), (cb,)), ((), ())), preferred_element_type=F32)


def trade(x, groups):
    return lax.all_to_all(x, ALL, 0, 0, axis_index_groups=groups)


def call(body, outs, *args, scratch=(), free=()):
    return pl.pallas_call(
        body,
        out_shape=[jax.ShapeDtypeStruct(s, d) for s, d in outs],
        in_specs=[pl.BlockSpec(memory_space=pltpu.VMEM)] * len(args),
        out_specs=[pl.BlockSpec(memory_space=pl.ANY if i in free else pltpu.VMEM) for i in range(len(outs))],
        scratch_shapes=list(scratch),
        compiler_params=pltpu.CompilerParams(vmem_limit_bytes=40 * 1024 * 1024),
    )(*args)


def is_core_0():
    return (lax.axis_index("rep") & 1) == 0


def left_half():
    return lax.broadcasted_iota(jnp.int32, (1, 128), 1) < 64


def total_of(got):
    total = got[0].astype(F32)
    for i in range(1, 8):
        total = total + got[i].astype(F32)
    return total


def sum_and_copy(got, cot, send):
    total, piece = total_of(got).astype(BF), cot[...]
    for u in E8:
        send[u, 0:128, :] = total
        send[u, 128:144, :] = piece


def update(got, gain_ref, w_in_ref, w_out_ref, out_ref, send, change, rows, columns, field, tiles, sems):
    summed = got[0, 0:128, :].astype(F32)
    for i in range(1, 8):
        summed = summed + got[i, 0:128, :].astype(F32)
    r = lax.axis_index("rows")
    first = is_core_0()
    u = label(jnp.where(first, r & 7, r >> 3))
    gain = gain_ref[...]
    w_in, w_out = w_in_ref[...], w_out_ref[...]
    cot = got[:, 128:144, :].reshape(128, 512)
    scale = lax.rsqrt(jnp.mean(summed * summed, axis=-1, keepdims=True) + 1e-05)
    normed = summed * scale
    lifted = (normed * gain).astype(BF)
    pre = dot(lifted, w_in, 1, 0)
    grad_hidden = dot(cot, w_out, 1, 1)
    sigma = jax.nn.sigmoid(pre)
    hidden = (pre * sigma).astype(BF)
    grad_pre = (grad_hidden * sigma * (1.0 + pre * (1.0 - sigma))).astype(BF)
    grad_lifted = dot(grad_pre, w_in, 1, 1)
    change[...] = dot(hidden, w_out, 1, 0).astype(BF)
    out_ref[...] = change[pl.ds(pl.multiple_of(u * 16, 16), 16), :]
    gain_row = jnp.sum(grad_lifted * normed, axis=0, keepdims=True)
    gain_high = gain_row.astype(BF).astype(F32)
    gain_rows = jnp.concatenate([jnp.zeros((14, 512), F32), gain_high, gain_row - gain_high], axis=0)
    grad_normed = grad_lifted * gain
    grad_summed = (
        scale * (grad_normed - normed * jnp.mean(grad_normed * normed, axis=-1, keepdims=True))
    ).astype(BF)
    field[...] = grad_summed
    copies = [pltpu.make_async_copy(field, send.at[v, 0:128], sems.at[v]) for v in E8]
    for copy in copies:
        copy.start()
    left = left_half()
    top = lax.broadcasted_iota(jnp.int32, (16, 1), 0) < 14

    def pairs(a, b, ref):
        a, b = a.astype(F32), b.astype(F32)
        for m in range(4):
            one, two = a[:, 128 * m : 128 * m + 128], b[:, 128 * m : 128 * m + 128]
            ref[2 * m] = jnp.where(left, one, pltpu.roll(two, 64, 1)).astype(BF)
            ref[2 * m + 1] = jnp.where(left, pltpu.roll(one, 64, 1), two).astype(BF)

    pairs(lifted, hidden, rows)
    pairs(grad_pre, cot, columns)
    for k in E8:
        tile = dot(rows[jnp.where(first, k, u)], columns[jnp.where(first, u, k)], 0, 0)
        tile = jnp.where(left, tile[0:64], tile[64:128])
        high = tile.astype(BF)
        low = tile - high.astype(F32)
        for j in range(4):
            at = slice(128 * j, 128 * j + 128)
            tiles[k, 0:16, at] = high[16 * j : 16 * j + 16]
            tiles[k, 16:32, at] = jnp.where(top, low[16 * j : 16 * j + 16], gain_rows[:, at]).astype(BF)
        copies.append(pltpu.make_async_copy(tiles.at[k], send.at[k, 128:160], sems.at[8 + k]))
        copies[-1].start()
    for copy in copies:
        copy.wait()


def back_and_tile(adjacency, got, nodes, change, send, out):
    own = nodes[pl.ds(pl.multiple_of(lax.axis_index("rep") * 16, 16), 16), :].astype(F32)
    final = (own + change[...].astype(F32)).astype(BF)
    for j in range(4):
        out[16 * j : 16 * j + 16, :] = final[:, 128 * j : 128 * j + 128]
    field = got[:, 0:128, :].reshape(1024, 512)
    back = dot(adjacency[...], field, 1, 0)
    for q in E8:
        for j in range(4):
            send[q, 16 * j : 16 * j + 16, :] = back[16 * q : 16 * q + 16, 128 * j : 128 * j + 128].astype(BF)
    exact, lows = jnp.zeros((16, 512), F32), jnp.zeros((16, 512), F32)
    for v in E8:
        exact = exact + got[v, 128:144, :].astype(F32)
        lows = lows + got[v, 144:160, :].astype(F32)
    exact = exact + jnp.where(lax.broadcasted_iota(jnp.int32, (16, 1), 0) < 14, lows, 0.0)
    gain = lows[14:15] + lows[15:16]
    gain = jnp.concatenate([gain[:, 128 * j : 128 * j + 128] for j in range(4)], axis=0)
    gain_high = gain.astype(BF).astype(F32)
    gain = jnp.concatenate([jnp.zeros((8, 128), F32), gain_high, gain - gain_high], axis=0)
    high = exact.astype(BF)
    low = exact - high.astype(F32)
    top = lax.broadcasted_iota(jnp.int32, (16, 1), 0) < 8
    for q in E8:
        for i in range(2):
            at = slice(128 * (2 * (q % 2) + i), 128 * (2 * (q % 2) + i) + 128)
            send[q, 64 + 16 * i : 80 + 16 * i, :] = high[:, at]
            send[q, 96 + 16 * i : 112 + 16 * i, :] = (low[:, at] if i == 0 else jnp.where(top, low[:, at], gain)).astype(BF)


def add_up(got, cotangent, out, piece, send, gain):
    total = total_of(got)
    own = cotangent[pl.ds(pl.multiple_of(lax.axis_index("rep") * 16, 16), 16), :].astype(F32)
    for j in range(4):
        piece[16 * j : 16 * j + 16, :] = (
            own[:, 128 * j : 128 * j + 128] + total[16 * j : 16 * j + 16]
        ).astype(BF)
    piece[64:128, :] = out[...]
    block = jnp.concatenate([total[64:88] + total[96:120], total[88:96]], axis=0).astype(BF)
    for r in range(64):
        send[r] = block
    for j in range(4):
        gain[0:1, 128 * j : 128 * j + 128] = total[120 + j : 121 + j] + total[124 + j : 125 + j]


def lay_rows(src, z, grad_in, grad_out):
    left = left_half()
    for m in range(4):
        even, odd = src[8 * z + 2 * m].astype(F32), src[8 * z + 2 * m + 1].astype(F32)
        cols = slice(128 * m, 128 * m + 128)
        grad_in[z, :, cols] = jnp.where(left, even, pltpu.roll(odd, 64, 1))
        grad_out[z, :, cols] = jnp.where(left, pltpu.roll(even, 64, 1), odd)


def lay(src, p0, p1, p2, p3, grad_in, grad_out, node_grad, node_out):
    for z in E8:
        lay_rows(src, z, grad_in, grad_out)
    p = lax.axis_index("rep")
    c = p & 1
    for d, pieces in enumerate((p0, p1, p2, p3)):
        for h in range(2):
            q = (((p >> 1) + 4 - d) & 3) * 2 + (c ^ h)
            rows = pl.ds(pl.multiple_of(16 * q, 16), 16)
            for j in range(4):
                cols = slice(128 * j, 128 * j + 128)
                node_grad[rows, cols] = pieces[h, 16 * j : 16 * j + 16, :]
                node_out[rows, cols] = pieces[h, 64 + 16 * j : 80 + 16 * j, :]


def lay_both(src, mine_in, mine_out, grad_in, grad_out, part_in, part_out, sems):
    c = lax.axis_index("rep") & 1
    copies = []

    def send(a, b, z, at):
        copies.append(pltpu.make_async_copy(a.at[z], b.at[z, at], sems.at[len(copies)]))
        copies[-1].start()

    for z in E8:
        send(mine_in, grad_in, z, c)
        send(mine_out, grad_out, z, c)
    for z in E8:
        lay_rows(src, z, part_in, part_out)
        send(part_in, grad_in, z, 1 - c)
        send(part_out, grad_out, z, 1 - c)
    for copy in copies:
        copy.wait()


def shards(nodes, adjacency, gain, w_in, w_out, cotangent):
    piece = lax.dynamic_slice_in_dim(cotangent, lax.axis_index("rep") * 16, 16, 0)
    cot = lax.ppermute(piece, ALL, OUT)

    part = dot(adjacency, nodes, 0, 0).astype(BF).reshape(8, 128, 512)
    (part,) = call(sum_and_copy, [((8, 144, 512), BF)], trade(part, ALONG_V), cot)
    got = trade(part, ALONG_U)

    change, send = call(
        update,
        [((16, 512), BF), ((8, 160, 512), BF)],
        got, gain.reshape(1, 512), w_in, w_out,
        scratch=[pltpu.VMEM((128, 512), BF)] + [pltpu.VMEM((8, 128, 128), BF)] * 2
        + [pltpu.VMEM((128, 512), BF), pltpu.VMEM((8, 32, 512), BF), pltpu.SemaphoreType.DMA((16,))],
        free=(1,),
    )
    change = lax.ppermute(change, ALL, BACK)
    send, out = call(
        back_and_tile, [((8, 128, 128), BF), ((64, 128), BF)],
        adjacency, trade(send, ALONG_V), nodes, change,
    )
    piece, send, grad_gain = call(
        add_up, [((128, 128), BF), ((64, 32, 128), BF), ((1, 512), F32)],
        lax.all_to_all(send, "rep", 0, 0), cotangent, out,
    )
    mine = trade(send, PLANES)
    pieces = jnp.stack([piece, lax.ppermute(piece, ALL, CORE)])
    pieces = [pieces] + [lax.ppermute(pieces, ALL, perm) for perm in SHIFT_X]
    mine, pieces = lax.optimization_barrier((mine, pieces))
    other = lax.ppermute(mine, ALL, CORE)
    half = ((8, 32, 512), F32)
    mine_in, mine_out, node_grad, node_out = call(
        lay, [half, half, ((128, 512), BF), ((128, 512), BF)], mine, *pieces
    )
    whole = jax.ShapeDtypeStruct((8, 2, 32, 512), F32)
    vmem = pl.BlockSpec(memory_space=pltpu.VMEM)
    grad_in, grad_out = pl.pallas_call(
        lay_both,
        out_shape=[whole, whole],
        in_specs=[vmem] * 3,
        out_specs=[pl.BlockSpec(memory_space=pl.ANY)] * 2,
        scratch_shapes=[pltpu.VMEM(*half)] * 2 + [pltpu.SemaphoreType.DMA((32,))],
        compiler_params=pltpu.CompilerParams(vmem_limit_bytes=40 * 1024 * 1024),
    )(other, mine_in, mine_out)
    return (node_out, node_grad, grad_in.reshape(512, 512), grad_out.reshape(512, 512), grad_gain.reshape(512))


def solution(mesh):
    return jax.shard_map(
        shards,
        mesh=mesh,
        in_specs=(P("rows", None), P("rows", "rep"), P(), P(), P(), P("rows", None)),
        out_specs=(P("rows", None), P("rows", None), P(), P(), P()),
        check_vma=False,
    )
```
